32 devices in a mesh: section: 8 (over y, x, core), uly: 4 (over z).
Axes of the slice: x: 2, y: 2, z: 4, core: 2. Of those that a mesh axis runs over, the one named last changes fastest.
Arguments:
- state: bfloat16 [8, 128, 3072], P('section', 'uly'), may hold values from -6 to 6
- patch_slot: int32 [8], replicated, may hold values from 0 to 3
- section_active: int32 [8], P('section'), may hold values from 1 to 2
- qkv_weight: bfloat16 [8, 3072, 3, 1536], P('section', None, None, 'uly'), may hold values from -0.109375 to 0.109375
- out_weight: bfloat16 [8, 1536, 3072], P('section', 'uly'), may hold values from -0.15625 to 0.15625
- norm_gain: bfloat16 [8, 3072], P('section'), may hold values from 0.099609375 to 1.8984375
- stale_keys: bfloat16 [8, 512, 1536], P('section', None, 'uly'), may hold values from -6 to 6
- stale_values: bfloat16 [8, 512, 1536], P('section', None, 'uly'), may hold values from -6 to 6
Outputs:
- final_state: bfloat16 [8, 128, 3072], P('section', 'uly')
The draws below stay inside these ranges and needn't reach their ends.
All inputs are finite; a program needn't handle non-finite values.
Results may differ from the reference program's by a relative error of at most 0.019.
Values may be sent and summed in bfloat16 or wider, within the bound.
No kernel may reach another device: no remote copies, remote signals or barrier semaphores. Data moves between devices by JAX's collectives and lax.ppermute only.
A program may use at most 64 MiB of HBM per device.

```python
import jax
import jax.numpy as jnp
from jax import lax

D = 3072
HEADS = 12
HD = 128
PT = 128
SLOTS = 4
TICKS = 3
SEQ = 512
N_SECTION = 8
N_ULY = 4


def touch_ends(values, rng, low, largest):
    index_at = [jax.random.randint(jax.random.fold_in(rng, axis), (), 0, length) for axis, length in enumerate(values.shape)]
    widest = values.shape.index(max(values.shape))
    neighbour = index_at[:widest] + [(index_at[widest] + 1) % values.shape[widest]] + index_at[widest + 1:]
    return values.at[tuple(index_at)].set(low).at[tuple(neighbour)].set(largest)


def block_levels(key, dims, shards, low, top_value):
    level, own = 1.0, jax.random.fold_in(key, 6)
    for axis_at, blocks in shards:
        draws = jnp.exp(jax.random.uniform(jax.random.fold_in(own, axis_at), (blocks,), jnp.float32, low / len(shards), top_value / len(shards)))
        level = level * jnp.repeat(draws, dims[axis_at] // blocks).reshape([-1 if axis == axis_at else 1 for axis in range(len(dims))])
    return level


def noise(stream_key, shape, deviation, bound, shards=(), dtype=jnp.bfloat16):
    array = jax.random.normal(stream_key, shape, jnp.float32) * deviation
    if len(shards) > 0:
        array = block_levels(stream_key, shape, shards, -0.22, 0.18) * array
    return jnp.clip(array, min=-bound, max=bound).astype(dtype)


def setup_inputs(seed: int = 0) -> dict:
    key_of = jax.random.split(jax.random.key(seed), 9)
    return {
        "state": noise(key_of[0], (N_SECTION, PT, D), 1.0, 6.0, ((0, 8), (1, 4))),
        "patch_slot": touch_ends(jax.random.randint(key_of[1], (N_SECTION,), 0, SLOTS), jax.random.fold_in(key_of[1], 1), 0, SLOTS - 1).astype(jnp.int32),
        "section_active": touch_ends(jax.random.randint(key_of[2], (N_SECTION,), 1, 3), jax.random.fold_in(key_of[2], 1), 1, 2).astype(jnp.int32),
        "qkv_weight": noise(key_of[3], (N_SECTION, D, 3, HEADS * HD), D ** -0.5, 0.109375, ((0, 8), (3, 4))),
        "out_weight": noise(key_of[4], (N_SECTION, HEADS * HD, D), (HEADS * HD) ** -0.5, 0.15625, ((0, 8), (1, 4))),
        "norm_gain": jnp.clip(1.0 + 0.18 * jax.random.normal(key_of[5], (N_SECTION, D), jnp.float32), 0.099609375, 1.8984375).astype(jnp.bfloat16),
        "stale_keys": noise(key_of[6], (N_SECTION, SEQ, HEADS * HD), 1.0, 6.0, ((0, 8), (2, 4))),
        "stale_values": noise(key_of[7], (N_SECTION, SEQ, HEADS * HD), 1.0, 6.0, ((0, 8), (2, 4))),
    }


def section_layer(current, qkv_weight, out_weight, norm_gain, key_cache, value_cache, patch_index):
    widened = current.astype(jnp.float32)
    mean_square = lax.optimization_barrier(jnp.mean(widened * widened, axis=-1, keepdims=True))
    normed = (widened * lax.rsqrt(mean_square + 1e-06) * norm_gain.astype(jnp.float32)).astype(jnp.bfloat16)
    projected = jnp.dot(normed, qkv_weight.reshape(D, 3 * HEADS * HD), preferred_element_type=jnp.float32)
    projected = projected.astype(jnp.bfloat16).reshape(PT, 3, HEADS * HD)
    row_start = (patch_index * PT).astype(jnp.int32)
    zero_index = jnp.zeros((), jnp.int32)
    key_cache = lax.dynamic_update_slice(key_cache, projected[:, 1], (row_start, zero_index))
    value_cache = lax.dynamic_update_slice(value_cache, projected[:, 2], (row_start, zero_index))
    query_heads = projected[:, 0].reshape(PT, HEADS, HD).astype(jnp.float32)
    key_heads = key_cache.reshape(SEQ, HEADS, HD).astype(jnp.float32)
    value_heads = value_cache.reshape(SEQ, HEADS, HD).astype(jnp.float32)
    scores = jnp.einsum('thd,shd->hts', query_heads, key_heads) * HD ** (-0.5)
    probs = jax.nn.softmax(scores, axis=-1).astype(jnp.bfloat16)
    attended = jnp.einsum('hts,shd->thd', probs.astype(jnp.float32), value_heads).astype(jnp.bfloat16)
    grouped = attended.reshape(PT, N_ULY, HEADS * HD // N_ULY).astype(jnp.float32)
    out_groups = out_weight.reshape(N_ULY, HEADS * HD // N_ULY, D).astype(jnp.float32)
    head_terms = jnp.einsum('tgf,gfd->gtd', grouped, out_groups).astype(jnp.bfloat16)
    head_total = lax.optimization_barrier(jnp.sum(head_terms.astype(jnp.float32), axis=0))
    updated = (widened + head_total).astype(jnp.bfloat16)
    return (updated, key_cache, value_cache)

def run_section(packed):
    current, qkv_weight, out_weight, norm_gain, key_cache, value_cache, patch_index, block_count = packed
    for pass_index in range(2):
        updated, new_keys, new_values = section_layer(current, qkv_weight, out_weight, norm_gain, key_cache, value_cache, patch_index)
        applies = block_count > pass_index
        current = jnp.where(applies, updated, current)
        key_cache = jnp.where(applies, new_keys, key_cache)
        value_cache = jnp.where(applies, new_values, value_cache)
    return (current, key_cache, value_cache)

def reference(state, patch_slot, section_active, qkv_weight, out_weight, norm_gain, stale_keys, stale_values):
    current = state
    key_cache = stale_keys
    value_cache = stale_values
    for tick_index in range(TICKS):
        patch_index = jnp.roll(patch_slot, tick_index)
        updated, key_cache, value_cache = lax.map(run_section, (current, qkv_weight, out_weight, norm_gain, key_cache, value_cache, patch_index, section_active))
        current = jnp.roll(updated, 1, axis=0)
    return current
```

```python
import functools

import jax
import jax.numpy as jnp
from jax import lax
from jax.experimental import pallas as pl
from jax.experimental.pallas import tpu as pltpu
from jax.sharding import PartitionSpec as P

HD = 128
TICKS = 3
PASSES = 2
SPLITS = 4


def block_kernel(chunks, info, *refs):
    mids = refs[:chunks]
    ends = refs[chunks:2 * chunks]
    gain, w_hbm, wo_hbm, kc_in, vc_in = refs[2 * chunks:2 * chunks + 5]
    outs = refs[2 * chunks + 5:]
    terms = outs[:chunks]
    kc, vc = outs[chunks:chunks + 2]
    w, wo, normed, attended, w_sems, wo_sem = outs[chunks + 2:]
    depth = w.shape[1]
    piece = depth // SPLITS
    rows = mids[0].shape[0]
    total_rows = rows * chunks
    heads = kc.shape[1] // HD
    applies = info[2] > 0

    @pl.when(applies)
    def _():
        copies = []
        for part in range(3):
            for i in range(SPLITS):
                span = pl.ds(i * piece, piece)
                copy = pltpu.make_async_copy(
                    w_hbm.at[part, span], w.at[part, span], w_sems.at[part, i]
                )
                copy.start()
                copies.append(copy)
        wo_copy = pltpu.make_async_copy(wo_hbm, wo, wo_sem)
        wo_copy.start()

        is_end = info[1] > 0
        gain_row = gain[...].astype(jnp.float32)
        for c in range(chunks):
            span = pl.ds(c * rows, rows)

            def put(ref, span=span):
                wide = ref[...].astype(jnp.float32)
                mean_square = jnp.mean(wide * wide, axis=-1, keepdims=True)
                normed[span, :] = (
                    wide * lax.rsqrt(mean_square + 1e-06) * gain_row
                ).astype(jnp.bfloat16)

            @pl.when(is_end)
            def _(put=put, c=c):
                put(ends[c])

            @pl.when(jnp.logical_not(is_end))
            def _(put=put, c=c):
                put(mids[c])

        parts = []
        for part in range(3):
            total = None
            for i in range(SPLITS):
                copies[part * SPLITS + i].wait()
                span = pl.ds(i * piece, piece)
                product = jnp.dot(
                    normed[:, span], w[part, span, :], preferred_element_type=jnp.float32
                )
                total = product if total is None else total + product
            parts.append(total.astype(jnp.bfloat16))
        query, key, value = parts
        start = pl.multiple_of(info[0], total_rows)
        kc[...] = kc_in[...]
        vc[...] = vc_in[...]
        kc[pl.ds(start, total_rows), :] = key
        vc[pl.ds(start, total_rows), :] = value
        for h in range(heads):
            cols = pl.ds(h * HD, HD)
            scores = lax.dot_general(
                query[:, h * HD:(h + 1) * HD],
                kc[:, cols],
                (((1,), (1,)), ((), ())),
                preferred_element_type=jnp.float32,
            ) * HD ** (-0.5)
            top = jnp.max(scores, axis=-1, keepdims=True)
            weights = jnp.exp(scores - top)
            probs = (weights / jnp.sum(weights, axis=-1, keepdims=True)).astype(jnp.bfloat16)
            attended[:, cols] = jnp.dot(
                probs, vc[:, cols], preferred_element_type=jnp.float32
            ).astype(jnp.bfloat16)
        wo_copy.wait()
        for c in range(chunks):
            terms[c][...] = jnp.dot(
                attended[pl.ds(c * rows, rows), :], wo[...], preferred_element_type=jnp.float32
            ).astype(jnp.bfloat16)

    @pl.when(jnp.logical_not(applies))
    def _():
        kc[...] = kc_in[...]
        vc[...] = vc_in[...]
        for c in range(chunks):
            terms[c][...] = jnp.zeros_like(terms[c])


def block_terms(info, mids, ends, gain, w, wo, kc, vc):
    chunks = len(mids)
    rows, width = mids[0].shape
    vmem = pl.BlockSpec(memory_space=pltpu.VMEM)
    hbm = pl.BlockSpec(memory_space=pl.ANY)
    row_count = rows * chunks
    flops = 2 * row_count * (w.size + wo.size + 2 * kc.size)
    out = pl.pallas_call(
        functools.partial(block_kernel, chunks),
        out_shape=[jax.ShapeDtypeStruct((rows, width), jnp.bfloat16)] * chunks
        + [jax.ShapeDtypeStruct(kc.shape, kc.dtype)] * 2,
        in_specs=[pl.BlockSpec(memory_space=pltpu.SMEM)]
        + [vmem] * (2 * chunks)
        + [vmem, hbm, hbm, vmem, vmem],
        out_specs=[vmem] * (chunks + 2),
        scratch_shapes=[
            pltpu.VMEM(w.shape, w.dtype),
            pltpu.VMEM(wo.shape, wo.dtype),
            pltpu.VMEM((row_count, width), jnp.bfloat16),
            pltpu.VMEM((row_count, kc.shape[1]), jnp.bfloat16),
            pltpu.SemaphoreType.DMA((3, SPLITS)),
            pltpu.SemaphoreType.DMA,
        ],
        compiler_params=pltpu.CompilerParams(vmem_limit_bytes=28 * 2**20),
        cost_estimate=pl.CostEstimate(
            flops=flops, bytes_accessed=2 * (w.size + wo.size), transcendentals=0
        ),
    )(info, *mids, *ends, gain, w, wo, kc, vc)
    return out[:chunks], out[chunks], out[chunks + 1]


def send(block, pairs, hop):
    sections = lax.axis_size("section")
    n = lax.axis_size("uly")
    route = [
        (s * n + a, (s + hop) % sections * n + b) for s in range(sections) for a, b in pairs
    ]
    return lax.ppermute(block, ("section", "uly"), route)


def added(*blocks):
    total = blocks[0].astype(jnp.float32)
    for block in blocks[1:]:
        total = total + block.astype(jnp.float32)
    return total.astype(jnp.bfloat16)


INWARD = ((0, 1), (3, 2))
ACROSS = ((1, 2), (2, 1))
OUTWARD = ((1, 0), (2, 3))
STAY = ((1, 1), (2, 2))


def gathered(own, place):
    n = lax.axis_size("uly")
    right, left = own, own
    from_left, from_right = [own], [own]
    for step in range(1, n):
        right = send(right, [(i, i + 1) for i in range(step - 1, n - 1)], 0)
        left = send(left, [(i, i - 1) for i in range(1, n - step + 1)], 0)
        from_left.append(right)
        from_right.append(left)
    shards_in_order = []
    for j in range(n):
        block = own
        for z in range(n):
            if z != j:
                other = from_left[z - j] if z > j else from_right[j - z]
                block = jnp.where(place == z, other, block)
        shards_in_order.append(block)
    return shards_in_order


def shards(
    state, patch_slot, section_active, qkv_weight, out_weight, norm_gain, stale_keys, stale_values
):
    section_count = lax.axis_size("section")
    section_index = lax.axis_index("section")
    place = lax.axis_index("uly")
    w = jnp.transpose(qkv_weight[0], (1, 0, 2))
    wo = out_weight[0]
    block_count = section_active[0]
    kc = stale_keys[0]
    vc = stale_values[0]
    patch_rows = state.shape[1] * lax.axis_size("uly")
    is_end = ((place == 0) | (place == 3)).astype(jnp.int32)
    lower = place <= 1
    mids = gathered(state[0], place)
    ends = mids
    for tick in range(TICKS):
        slot = patch_slot[(section_index - tick) % section_count]
        for index in range(PASSES):
            applies = block_count > index
            info = jnp.stack([slot * patch_rows, is_end, applies.astype(jnp.int32)])
            terms, kc, vc = block_terms(info, mids, ends, norm_gain, w, wo, kc, vc)
            last = index == PASSES - 1
            if last and tick == TICKS - 1:
                sums = [None] * 4
                for c in (0, 3, 1, 2):
                    sums[c] = added(terms[c], send(terms[c], INWARD, 0))
                results = []
                for near, far in ((0, 3), (1, 2)):
                    arrived = send(jnp.where(lower, sums[far], sums[near]), ACROSS, 0)
                    own = jnp.where(lower, sums[near], sums[far])
                    before = jnp.where(lower, mids[near], mids[far])
                    after = jnp.where(applies, added(before, own, arrived), before)
                    results.append(send(after, OUTWARD if near == 0 else STAY, 1))
                return jnp.where(is_end > 0, results[0], results[1])[None]
            next_mids, next_ends = [], []
            for c in range(len(terms)):
                inner = added(terms[c], send(terms[c], INWARD, 0))
                arrived = send(inner, ACROSS, 0)
                after = jnp.where(applies, added(mids[c], inner, arrived), mids[c])
                next_ends.append(send(after, OUTWARD, 1 if last else 0))
                next_mids.append(send(after, STAY, 1) if last else after)
            mids, ends = next_mids, next_ends


def solution(mesh):
    return jax.shard_map(
        shards,
        mesh=mesh,
        in_specs=(
            P("section", "uly", None),
            P(),
            P("section"),
            P("section", None, None, "uly"),
            P("section", "uly", None),
            P("section", None),
            P("section", None, "uly"),
            P("section", None, "uly"),
        ),
        out_specs=P("section", "uly", None),
        check_vma=False,
    )
```

```python
import functools

import jax
import jax.numpy as jnp
from jax import lax
from jax.experimental import pallas as pl
from jax.experimental.pallas import tpu as pltpu
from jax.sharding import PartitionSpec as P

HD = 128
TICKS = 3
PASSES = 2
VMEM_LIMIT = 24 * 2**20


def block_kernel(chunks, info, *refs):
    mids = refs[:chunks]
    ends = refs[chunks:2 * chunks]
    gain, w, wo, kc_in, vc_in = refs[2 * chunks:2 * chunks + 5]
    outs = refs[2 * chunks + 5:]
    terms = outs[:chunks]
    kc, vc, normed, attended = outs[chunks:]
    rows = mids[0].shape[0]
    total_rows = rows * chunks
    heads = kc.shape[1] // HD
    applies = info[2] > 0

    @pl.when(applies)
    def _():
        is_end = info[1] > 0
        gain_row = gain[...].astype(jnp.float32)
        for c in range(chunks):
            span = pl.ds(c * rows, rows)

            def put(ref, span=span):
                wide = ref[...].astype(jnp.float32)
                mean_square = jnp.mean(wide * wide, axis=-1, keepdims=True)
                normed[span, :] = (
                    wide * lax.rsqrt(mean_square + 1e-06) * gain_row
                ).astype(jnp.bfloat16)

            @pl.when(is_end)
            def _(put=put, c=c):
                put(ends[c])

            @pl.when(jnp.logical_not(is_end))
            def _(put=put, c=c):
                put(mids[c])

        query, key, value = [
            jnp.dot(normed[...], w[part], preferred_element_type=jnp.float32).astype(jnp.bfloat16)
            for part in range(3)
        ]
        start = pl.multiple_of(info[0], total_rows)
        kc[pl.ds(start, total_rows), :] = key
        vc[pl.ds(start, total_rows), :] = value
        for h in range(heads):
            cols = pl.ds(h * HD, HD)
            scores = lax.dot_general(
                query[:, h * HD:(h + 1) * HD],
                kc[:, cols],
                (((1,), (1,)), ((), ())),
                preferred_element_type=jnp.float32,
            ) * HD ** (-0.5)
            top = jnp.max(scores, axis=-1, keepdims=True)
            weights = jnp.exp(scores - top)
            probs = (weights / jnp.sum(weights, axis=-1, keepdims=True)).astype(jnp.bfloat16)
            attended[:, cols] = jnp.dot(
                probs, vc[:, cols], preferred_element_type=jnp.float32
            ).astype(jnp.bfloat16)
        for c in range(chunks):
            terms[c][...] = jnp.dot(
                attended[pl.ds(c * rows, rows), :], wo[...], preferred_element_type=jnp.float32
            ).astype(jnp.bfloat16)


def load_kernel(*refs):
    count = len(refs) // 2
    sems = refs[-1]
    pairs = list(zip(refs[:count], refs[count:2 * count]))
    copies = [pltpu.make_async_copy(a, b, sems.at[i]) for i, (a, b) in enumerate(pairs)]
    for copy in copies:
        copy.start()
    for copy in copies:
        copy.wait()


def loaded(*arrays):
    return pl.pallas_call(
        load_kernel,
        out_shape=[pltpu.VMEM(a.shape, a.dtype) for a in arrays],
        in_specs=[pl.BlockSpec(memory_space=pl.ANY)] * len(arrays),
        out_specs=[pl.BlockSpec(memory_space=pltpu.VMEM)] * len(arrays),
        scratch_shapes=[pltpu.SemaphoreType.DMA((len(arrays),))],
        compiler_params=pltpu.CompilerParams(vmem_limit_bytes=VMEM_LIMIT),
        cost_estimate=pl.CostEstimate(
            flops=0, bytes_accessed=2 * sum(a.size for a in arrays), transcendentals=0
        ),
    )(*[pltpu.with_memory_space_constraint(a, pltpu.HBM) for a in arrays])


def block_terms(info, mids, ends, gain, w, wo, kc, vc):
    chunks = len(mids)
    rows, width = mids[0].shape
    vmem = pl.BlockSpec(memory_space=pltpu.VMEM)
    row_count = rows * chunks
    flops = 2 * row_count * (w.size + wo.size + 2 * kc.size)
    held = [pltpu.with_memory_space_constraint(x, pltpu.VMEM) for x in (w, wo, kc, vc)]
    cache = pltpu.VMEM(kc.shape, kc.dtype)
    out = pl.pallas_call(
        functools.partial(block_kernel, chunks),
        out_shape=[jax.ShapeDtypeStruct((rows, width), jnp.bfloat16)] * chunks + [cache] * 2,
        in_specs=[pl.BlockSpec(memory_space=pltpu.SMEM)] + [vmem] * (2 * chunks + 5),
        out_specs=[vmem] * (chunks + 2),
        input_output_aliases={2 * chunks + 4: chunks, 2 * chunks + 5: chunks + 1},
        scratch_shapes=[
            pltpu.VMEM((row_count, width), jnp.bfloat16),
            pltpu.VMEM((row_count, kc.shape[1]), jnp.bfloat16),
        ],
        compiler_params=pltpu.CompilerParams(vmem_limit_bytes=VMEM_LIMIT),
        cost_estimate=pl.CostEstimate(
            flops=flops, bytes_accessed=2 * (w.size + wo.size), transcendentals=0
        ),
    )(info, *mids, *ends, gain, *held)
    return out[:chunks], out[chunks], out[chunks + 1]


def send(block, pairs, hop):
    sections = lax.axis_size("section")
    n = lax.axis_size("uly")
    route = [
        (s * n + a, (s + hop) % sections * n + b) for s in range(sections) for a, b in pairs
    ]
    return lax.ppermute(block, ("section", "uly"), route)


def added(*blocks):
    total = blocks[0].astype(jnp.float32)
    for block in blocks[1:]:
        total = total + block.astype(jnp.float32)
    return total.astype(jnp.bfloat16)


INWARD = ((0, 1), (3, 2))
ACROSS = ((1, 2), (2, 1))
OUTWARD = ((1, 0), (2, 3))
STAY = ((1, 1), (2, 2))


def behind(block, *others):
    return lax.optimization_barrier((block, *others))[0]


def gathered(own, place):
    n = lax.axis_size("uly")
    turned = [own] + [send(own, [(i, (i + k) % n) for i in range(n)], 0) for k in range(1, n)]
    shards_in_order = []
    for j in range(n):
        block = turned[0]
        for k in range(1, n):
            block = jnp.where((place - k) % n == j, turned[k], block)
        shards_in_order.append(block)
    return shards_in_order


def shards(
    state, patch_slot, section_active, qkv_weight, out_weight, norm_gain, stale_keys, stale_values
):
    section_count = lax.axis_size("section")
    section_index = lax.axis_index("section")
    place = lax.axis_index("uly")
    w = jnp.transpose(qkv_weight[0], (1, 0, 2))
    wo = out_weight[0]
    block_count = section_active[0]
    w, wo, kc, vc = loaded(w, wo, stale_keys[0], stale_values[0])
    patch_rows = state.shape[1] * lax.axis_size("uly")
    is_end = ((place == 0) | (place == 3)).astype(jnp.int32)
    lower = place <= 1
    mids = gathered(state[0], place)
    ends = mids
    for tick in range(TICKS):
        slot = patch_slot[(section_index - tick) % section_count]
        for index in range(PASSES):
            applies = block_count > index
            info = jnp.stack([slot * patch_rows, is_end, applies.astype(jnp.int32)])
            terms, kc, vc = block_terms(info, mids, ends, norm_gain, w, wo, kc, vc)
            last = index == PASSES - 1
            if last and tick == TICKS - 1:
                sums = [None] * 4
                for c in (0, 3, 1, 2):
                    sums[c] = added(terms[c], send(terms[c], INWARD, 0))
                results = []
                for near, far in ((0, 3), (1, 2)):
                    arrived = send(jnp.where(lower, sums[far], sums[near]), ACROSS, 0)
                    own = jnp.where(lower, sums[near], sums[far])
                    before = jnp.where(lower, mids[near], mids[far])
                    after = jnp.where(applies, added(before, own, arrived), before)
                    results.append(send(after, OUTWARD if near == 0 else STAY, 1))
                return jnp.where(is_end > 0, results[0], results[1])[None]
            count = len(terms)
            next_mids, next_ends = [None] * count, [None] * count
            firsts, inners, seconds = [None] * count, [None] * count, [None] * count
            for step in range(count + 2):
                c = step
                if c < count:
                    block = terms[c] if c < 2 else behind(terms[c], inners[c - 2])
                    firsts[c] = send(block, INWARD, 0)
                c = step - 1
                if 0 <= c < count:
                    arrived = firsts[c] if c < 2 else behind(firsts[c], next_mids[c - 2])
                    inners[c] = added(terms[c], arrived)
                    seconds[c] = send(inners[c], ACROSS, 0)
                c = step - 2
                if 0 <= c < count:
                    updated = added(mids[c], inners[c], seconds[c])
                    updated = jnp.where(applies, updated, mids[c])
                    next_ends[c] = send(updated, OUTWARD, 1 if last else 0)
                    next_mids[c] = updated
            if last:
                next_mids = [
                    send(
                        behind(next_mids[c], next_mids[c + 1] if c + 2 < count else next_ends[c - 1]),
                        STAY,
                        1,
                    )
                    for c in range(count)
                ]
            mids, ends = next_mids, next_ends


def solution(mesh):
    return jax.shard_map(
        shards,
        mesh=mesh,
        in_specs=(
            P("section", "uly", None),
            P(),
            P("section"),
            P("section", None, None, "uly"),
            P("section", "uly", None),
            P("section", None),
            P("section", None, "uly"),
            P("section", None, "uly"),
        ),
        out_specs=P("section", "uly", None),
        check_vma=False,
    )
```

```python
import functools

import jax
import jax.numpy as jnp
from jax import lax
from jax.experimental import pallas as pl
from jax.experimental.pallas import tpu as pltpu
from jax.sharding import PartitionSpec as P

HD = 128
TICKS = 3
PASSES = 2
VMEM_LIMIT = 24 * 2**20


def block_kernel(chunks, info, *refs):
    blocks = refs[:chunks]
    gain, w, wo, _, _ = refs[chunks:chunks + 5]
    terms = refs[chunks + 5:2 * chunks + 5]
    kc, vc, normed, attended = refs[2 * chunks + 5:]
    rows = blocks[0].shape[0]
    total_rows = rows * chunks
    heads = kc.shape[1] // HD

    @pl.when(info[1] > 0)
    def _():
        gain_row = gain[...].astype(jnp.float32)
        for c in range(chunks):
            wide = blocks[c][...].astype(jnp.float32)
            mean_square = jnp.mean(wide * wide, axis=-1, keepdims=True)
            normed[pl.ds(c * rows, rows), :] = (
                wide * lax.rsqrt(mean_square + 1e-06) * gain_row
            ).astype(jnp.bfloat16)
        query, key, value = [
            jnp.dot(normed[...], w[part], preferred_element_type=jnp.float32).astype(jnp.bfloat16)
            for part in range(3)
        ]
        start = pl.multiple_of(info[0], total_rows)
        kc[pl.ds(start, total_rows), :] = key
        vc[pl.ds(start, total_rows), :] = value
        for h in range(heads):
            cols = pl.ds(h * HD, HD)
            scores = lax.dot_general(
                query[:, h * HD:(h + 1) * HD],
                kc[:, cols],
                (((1,), (1,)), ((), ())),
                preferred_element_type=jnp.float32,
            ) * HD ** (-0.5)
            top = jnp.max(scores, axis=-1, keepdims=True)
            weights = jnp.exp(scores - top)
            probs = (weights / jnp.sum(weights, axis=-1, keepdims=True)).astype(jnp.bfloat16)
            attended[:, cols] = jnp.dot(
                probs, vc[:, cols], preferred_element_type=jnp.float32
            ).astype(jnp.bfloat16)
        for c in range(chunks):
            terms[c][...] = jnp.dot(
                attended[pl.ds(c * rows, rows), :], wo[...], preferred_element_type=jnp.float32
            ).astype(jnp.bfloat16)


def load_kernel(*refs):
    count = len(refs) // 2
    sems = refs[-1]
    pairs = list(zip(refs[:count], refs[count:2 * count]))
    copies = [pltpu.make_async_copy(a, b, sems.at[i]) for i, (a, b) in enumerate(pairs)]
    for copy in copies:
        copy.start()
    for copy in copies:
        copy.wait()


def loaded(*arrays):
    return pl.pallas_call(
        load_kernel,
        out_shape=[pltpu.VMEM(a.shape, a.dtype) for a in arrays],
        in_specs=[pl.BlockSpec(memory_space=pl.ANY)] * len(arrays),
        out_specs=[pl.BlockSpec(memory_space=pltpu.VMEM)] * len(arrays),
        scratch_shapes=[pltpu.SemaphoreType.DMA((len(arrays),))],
        compiler_params=pltpu.CompilerParams(vmem_limit_bytes=VMEM_LIMIT),
        cost_estimate=pl.CostEstimate(
            flops=0, bytes_accessed=2 * sum(a.size for a in arrays), transcendentals=0
        ),
    )(*[pltpu.with_memory_space_constraint(a, pltpu.HBM) for a in arrays])


def block_terms(info, blocks, gain, w, wo, kc, vc):
    chunks = len(blocks)
    rows, width = blocks[0].shape
    vmem = pl.BlockSpec(memory_space=pltpu.VMEM)
    row_count = rows * chunks
    flops = 2 * row_count * (w.size + wo.size + 2 * kc.size)
    held = [pltpu.with_memory_space_constraint(x, pltpu.VMEM) for x in (w, wo, kc, vc)]
    cache = pltpu.VMEM(kc.shape, kc.dtype)
    out = pl.pallas_call(
        functools.partial(block_kernel, chunks),
        out_shape=[jax.ShapeDtypeStruct((rows, width), jnp.bfloat16)] * chunks + [cache] * 2,
        in_specs=[pl.BlockSpec(memory_space=pltpu.SMEM)] + [vmem] * (chunks + 5),
        out_specs=[vmem] * (chunks + 2),
        input_output_aliases={chunks + 4: chunks, chunks + 5: chunks + 1},
        scratch_shapes=[
            pltpu.VMEM((row_count, width), jnp.bfloat16),
            pltpu.VMEM((row_count, kc.shape[1]), jnp.bfloat16),
        ],
        compiler_params=pltpu.CompilerParams(vmem_limit_bytes=VMEM_LIMIT),
        cost_estimate=pl.CostEstimate(
            flops=flops, bytes_accessed=2 * (w.size + wo.size), transcendentals=0
        ),
    )(info, *blocks, gain, *held)
    return out[:chunks], out[chunks], out[chunks + 1]


def send(block, turn, hop):
    sections = lax.axis_size("section")
    n = lax.axis_size("uly")
    route = [
        (s * n + i, (s + hop) % sections * n + (i + turn) % n)
        for s in range(sections)
        for i in range(n)
    ]
    return lax.ppermute(block, ("section", "uly"), route)


def gathered(own, hop):
    n = lax.axis_size("uly")
    first = own if hop == 0 else send(own, 0, hop)
    return [first] + [send(own, k, hop) for k in range(1, n)]


def summed(blocks):
    total = blocks[0].astype(jnp.float32)
    for block in blocks[1:]:
        total = total + block.astype(jnp.float32)
    return total


def shards(
    state, patch_slot, section_active, qkv_weight, out_weight, norm_gain, stale_keys, stale_values
):
    section_count = lax.axis_size("section")
    section_index = lax.axis_index("section")
    w = jnp.transpose(qkv_weight[0], (1, 0, 2))
    wo = out_weight[0]
    w, wo, kc, vc = loaded(w, wo, stale_keys[0], stale_values[0])
    block_count = section_active[0]
    n = lax.axis_size("uly")
    patch_rows = state.shape[1] * n
    own = state[0]
    blocks = gathered(own, 0)
    for tick in range(TICKS):
        slot = patch_slot[(section_index - tick) % section_count]
        for index in range(PASSES):
            applies = block_count > index
            info = jnp.stack([slot * patch_rows, applies.astype(jnp.int32)])
            terms, kc, vc = block_terms(info, blocks, norm_gain, w, wo, kc, vc)
            arrived = [send(terms[k], n - k, 0) for k in range(1, n)]
            updated = own.astype(jnp.float32) + summed([terms[0]] + arrived)
            updated = jnp.where(applies, updated.astype(jnp.bfloat16), own)
            last = index == PASSES - 1
            if last and tick == TICKS - 1:
                return send(updated, 0, 1)[None]
            blocks = gathered(updated, 1 if last else 0)
            own = blocks[0]


def solution(mesh):
    return jax.shard_map(
        shards,
        mesh=mesh,
        in_specs=(
            P("section", "uly", None),
            P(),
            P("section"),
            P("section", None, None, "uly"),
            P("section", "uly", None),
            P("section", None),
            P("section", None, "uly"),
            P("section", None, "uly"),
        ),
        out_specs=P("section", "uly", None),
        check_vma=False,
    )
```

```python
import functools

import jax
import jax.numpy as jnp
from jax import lax
from jax.experimental import pallas as pl
from jax.experimental.pallas import tpu as pltpu
from jax.sharding import PartitionSpec as P

HD = 128
TICKS = 3
PASSES = 2
VMEM_LIMIT = 24 * 2**20


def block_kernel(chunks, info, *refs):
    blocks = refs[:chunks]
    gain, w, wo, _, _ = refs[chunks:chunks + 5]
    terms = refs[chunks + 5:2 * chunks + 5]
    kc, vc, normed, attended = refs[2 * chunks + 5:]
    rows = blocks[0].shape[0]
    total_rows = rows * chunks
    heads = kc.shape[1] // HD

    @pl.when(info[1] > 0)
    def _():
        gain_row = gain[...].astype(jnp.float32)
        for c in range(chunks):
            wide = blocks[c][...].astype(jnp.float32)
            mean_square = jnp.mean(wide * wide, axis=-1, keepdims=True)
            normed[pl.ds(c * rows, rows), :] = (
                wide * lax.rsqrt(mean_square + 1e-06) * gain_row
            ).astype(jnp.bfloat16)
        query, key, value = [
            jnp.dot(normed[...], w[part], preferred_element_type=jnp.float32).astype(jnp.bfloat16)
            for part in range(3)
        ]
        start = pl.multiple_of(info[0], total_rows)
        kc[pl.ds(start, total_rows), :] = key
        vc[pl.ds(start, total_rows), :] = value
        for h in range(heads):
            cols = pl.ds(h * HD, HD)
            scores = lax.dot_general(
                query[:, h * HD:(h + 1) * HD],
                kc[:, cols],
                (((1,), (1,)), ((), ())),
                preferred_element_type=jnp.float32,
            ) * HD ** (-0.5)
            top = jnp.max(scores, axis=-1, keepdims=True)
            weights = jnp.exp(scores - top)
            probs = (weights / jnp.sum(weights, axis=-1, keepdims=True)).astype(jnp.bfloat16)
            attended[:, cols] = jnp.dot(
                probs, vc[:, cols], preferred_element_type=jnp.float32
            ).astype(jnp.bfloat16)
        for c in range(chunks):
            terms[c][...] = jnp.dot(
                attended[pl.ds(c * rows, rows), :], wo[...], preferred_element_type=jnp.float32
            ).astype(jnp.bfloat16)


def load_kernel(*refs):
    count = len(refs) // 2
    sems = refs[-1]
    pairs = list(zip(refs[:count], refs[count:2 * count]))
    copies = [pltpu.make_async_copy(a, b, sems.at[i]) for i, (a, b) in enumerate(pairs)]
    for copy in copies:
        copy.start()
    for copy in copies:
        copy.wait()


def loaded(*arrays):
    return pl.pallas_call(
        load_kernel,
        out_shape=[pltpu.VMEM(a.shape, a.dtype) for a in arrays],
        in_specs=[pl.BlockSpec(memory_space=pl.ANY)] * len(arrays),
        out_specs=[pl.BlockSpec(memory_space=pltpu.VMEM)] * len(arrays),
        scratch_shapes=[pltpu.SemaphoreType.DMA((len(arrays),))],
        compiler_params=pltpu.CompilerParams(vmem_limit_bytes=VMEM_LIMIT),
        cost_estimate=pl.CostEstimate(
            flops=0, bytes_accessed=2 * sum(a.size for a in arrays), transcendentals=0
        ),
    )(*[pltpu.with_memory_space_constraint(a, pltpu.HBM) for a in arrays])


def block_terms(info, blocks, gain, w, wo, kc, vc):
    chunks = len(blocks)
    rows, width = blocks[0].shape
    vmem = pl.BlockSpec(memory_space=pltpu.VMEM)
    row_count = rows * chunks
    flops = 2 * row_count * (w.size + wo.size + 2 * kc.size)
    held = [pltpu.with_memory_space_constraint(x, pltpu.VMEM) for x in (w, wo, kc, vc)]
    cache = pltpu.VMEM(kc.shape, kc.dtype)
    out = pl.pallas_call(
        functools.partial(block_kernel, chunks),
        out_shape=[jax.ShapeDtypeStruct((rows, width), jnp.bfloat16)] * chunks + [cache] * 2,
        in_specs=[pl.BlockSpec(memory_space=pltpu.SMEM)] + [vmem] * (chunks + 5),
        out_specs=[vmem] * (chunks + 2),
        input_output_aliases={chunks + 4: chunks, chunks + 5: chunks + 1},
        scratch_shapes=[
            pltpu.VMEM((row_count, width), jnp.bfloat16),
            pltpu.VMEM((row_count, kc.shape[1]), jnp.bfloat16),
        ],
        compiler_params=pltpu.CompilerParams(vmem_limit_bytes=VMEM_LIMIT),
        cost_estimate=pl.CostEstimate(
            flops=flops, bytes_accessed=2 * (w.size + wo.size), transcendentals=0
        ),
    )(info, *blocks, gain, *held)
    return out[:chunks], out[chunks], out[chunks + 1]


STAY = ((0, 0), (1, 1), (2, 2), (3, 3))
SWAP = ((0, 1), (1, 0), (2, 3), (3, 2))
MID = ((0, 0), (1, 2), (2, 1), (3, 3))
INWARD = ((0, 2), (3, 1), (1, 0), (2, 3))
OUTWARD = ((2, 0), (1, 3), (0, 1), (3, 2))


def send(block, pairs, hop=0):
    sections = lax.axis_size("section")
    n = lax.axis_size("uly")
    route = [
        (s * n + a, (s + hop) % sections * n + b) for s in range(sections) for a, b in pairs
    ]
    return lax.ppermute(block, ("section", "uly"), route)


def summed(*blocks):
    total = blocks[0].astype(jnp.float32)
    for block in blocks[1:]:
        total = total + block.astype(jnp.float32)
    return total


def gathered(own, at_end, hop=0):
    partner = send(own, SWAP, hop)
    across = send(own, MID, hop)
    first = send(own, STAY, hop) if hop else own
    far = send(partner, OUTWARD)
    far_mid = send(partner, MID)
    near = send(across, SWAP)
    return [first, partner, jnp.where(at_end, near, across), jnp.where(at_end, far, far_mid)]


def scattered(terms, at_end):
    own, partner, near, far = terms
    far_in = send(far, INWARD)
    far_mid = send(far, MID)
    near_in = send(near, SWAP)
    passed = summed(partner, far_in, far_mid).astype(jnp.bfloat16)
    from_pair = send(jnp.where(at_end, partner, passed), SWAP)
    from_across = send(summed(near, near_in).astype(jnp.bfloat16), MID)
    total = summed(own, from_pair)
    return jnp.where(at_end, total, total + from_across.astype(jnp.float32))


def shards(
    state, patch_slot, section_active, qkv_weight, out_weight, norm_gain, stale_keys, stale_values
):
    section_count = lax.axis_size("section")
    section_index = lax.axis_index("section")
    w = jnp.transpose(qkv_weight[0], (1, 0, 2))
    wo = out_weight[0]
    w, wo, kc, vc = loaded(w, wo, stale_keys[0], stale_values[0])
    block_count = section_active[0]
    n = lax.axis_size("uly")
    patch_rows = state.shape[1] * n
    own = state[0]
    place = lax.axis_index("uly")
    at_end = (place == 0) | (place == n - 1)
    blocks = gathered(own, at_end)
    for tick in range(TICKS):
        slot = patch_slot[(section_index - tick) % section_count]
        for index in range(PASSES):
            applies = block_count > index
            info = jnp.stack([slot * patch_rows, applies.astype(jnp.int32)])
            terms, kc, vc = block_terms(info, blocks, norm_gain, w, wo, kc, vc)
            updated = own.astype(jnp.float32) + scattered(terms, at_end)
            updated = jnp.where(applies, updated.astype(jnp.bfloat16), own)
            last = index == PASSES - 1
            if last and tick == TICKS - 1:
                return send(updated, STAY, 1)[None]
            blocks = gathered(updated, at_end, 1 if last else 0)
            own = blocks[0]


def solution(mesh):
    return jax.shard_map(
        shards,
        mesh=mesh,
        in_specs=(
            P("section", "uly", None),
            P(),
            P("section"),
            P("section", None, None, "uly"),
            P("section", "uly", None),
            P("section", None),
            P("section", None, "uly"),
            P("section", None, "uly"),
        ),
        out_specs=P("section", "uly", None),
        check_vma=False,
    )
```

```python
import functools

import jax
import jax.numpy as jnp
from jax import lax
from jax.experimental import pallas as pl
from jax.experimental.pallas import tpu as pltpu
from jax.sharding import PartitionSpec as P

HD = 128
TICKS = 3
PASSES = 2
VMEM_LIMIT = 24 * 2**20


def block_kernel(chunks, info, *refs):
    blocks = refs[:chunks]
    gain, w, wo, _, _ = refs[chunks:chunks + 5]
    terms = refs[chunks + 5:2 * chunks + 5]
    kc, vc, normed, attended = refs[2 * chunks + 5:]
    rows = blocks[0].shape[0]
    total_rows = rows * chunks
    heads = kc.shape[1] // HD

    @pl.when(info[1] > 0)
    def _():
        gain_row = gain[...].astype(jnp.float32)
        for c in range(chunks):
            wide = blocks[c][...].astype(jnp.float32)
            mean_square = jnp.mean(wide * wide, axis=-1, keepdims=True)
            normed[pl.ds(c * rows, rows), :] = (
                wide * lax.rsqrt(mean_square + 1e-06) * gain_row
            ).astype(jnp.bfloat16)
        query, key, value = [
            jnp.dot(normed[...], w[part], preferred_element_type=jnp.float32).astype(jnp.bfloat16)
            for part in range(3)
        ]
        start = pl.multiple_of(info[0], total_rows)
        kc[pl.ds(start, total_rows), :] = key
        vc[pl.ds(start, total_rows), :] = value
        for h in range(heads):
            cols = pl.ds(h * HD, HD)
            scores = lax.dot_general(
                query[:, h * HD:(h + 1) * HD],
                kc[:, cols],
                (((1,), (1,)), ((), ())),
                preferred_element_type=jnp.float32,
            ) * HD ** (-0.5)
            top = jnp.max(scores, axis=-1, keepdims=True)
            weights = jnp.exp(scores - top)
            probs = (weights / jnp.sum(weights, axis=-1, keepdims=True)).astype(jnp.bfloat16)
            attended[:, cols] = jnp.dot(
                probs, vc[:, cols], preferred_element_type=jnp.float32
            ).astype(jnp.bfloat16)
        for c in range(chunks):
            terms[c][...] = jnp.dot(
                attended[pl.ds(c * rows, rows), :], wo[...], preferred_element_type=jnp.float32
            ).astype(jnp.bfloat16)


def load_kernel(*refs):
    count = len(refs) // 2
    sems = refs[-1]
    pairs = list(zip(refs[:count], refs[count:2 * count]))
    copies = [pltpu.make_async_copy(a, b, sems.at[i]) for i, (a, b) in enumerate(pairs)]
    for copy in copies:
        copy.start()
    for copy in copies:
        copy.wait()


def loaded(*arrays):
    return pl.pallas_call(
        load_kernel,
        out_shape=[pltpu.VMEM(a.shape, a.dtype) for a in arrays],
        in_specs=[pl.BlockSpec(memory_space=pl.ANY)] * len(arrays),
        out_specs=[pl.BlockSpec(memory_space=pltpu.VMEM)] * len(arrays),
        scratch_shapes=[pltpu.SemaphoreType.DMA((len(arrays),))],
        compiler_params=pltpu.CompilerParams(vmem_limit_bytes=VMEM_LIMIT),
        cost_estimate=pl.CostEstimate(
            flops=0, bytes_accessed=2 * sum(a.size for a in arrays), transcendentals=0
        ),
    )(*[pltpu.with_memory_space_constraint(a, pltpu.HBM) for a in arrays])


def block_terms(info, blocks, gain, w, wo, kc, vc):
    chunks = len(blocks)
    rows, width = blocks[0].shape
    vmem = pl.BlockSpec(memory_space=pltpu.VMEM)
    row_count = rows * chunks
    flops = 2 * row_count * (w.size + wo.size + 2 * kc.size)
    held = [pltpu.with_memory_space_constraint(x, pltpu.VMEM) for x in (w, wo, kc, vc)]
    cache = pltpu.VMEM(kc.shape, kc.dtype)
    out = pl.pallas_call(
        functools.partial(block_kernel, chunks),
        out_shape=[jax.ShapeDtypeStruct((rows, width), jnp.bfloat16)] * chunks + [cache] * 2,
        in_specs=[pl.BlockSpec(memory_space=pltpu.SMEM)] + [vmem] * (chunks + 5),
        out_specs=[vmem] * (chunks + 2),
        input_output_aliases={chunks + 4: chunks, chunks + 5: chunks + 1},
        scratch_shapes=[
            pltpu.VMEM((row_count, width), jnp.bfloat16),
            pltpu.VMEM((row_count, kc.shape[1]), jnp.bfloat16),
        ],
        compiler_params=pltpu.CompilerParams(vmem_limit_bytes=VMEM_LIMIT),
        cost_estimate=pl.CostEstimate(
            flops=flops, bytes_accessed=2 * (w.size + wo.size), transcendentals=0
        ),
    )(info, *blocks, gain, *held)
    return out[:chunks], out[chunks], out[chunks + 1]


STAY = ((0, 0), (1, 1), (2, 2), (3, 3))
NEAR = ((0, 1), (1, 0), (2, 3), (3, 2))
FAR = ((0, 3), (1, 2), (2, 1), (3, 0))


def send(block, pairs, hop=0):
    sections = lax.axis_size("section")
    n = lax.axis_size("uly")
    route = [
        (s * n + a, (s + hop) % sections * n + b) for s in range(sections) for a, b in pairs
    ]
    return lax.ppermute(block, ("section", "uly"), route)


def summed(*blocks):
    total = blocks[0].astype(jnp.float32)
    for block in blocks[1:]:
        total = total + block.astype(jnp.float32)
    return total


def gathered(own, hop=0):
    far = send(own, FAR, hop)
    near = send(own, NEAR, hop)
    first = send(own, STAY, hop) if hop else own
    return [first, near, far, send(far, NEAR)]


def scattered(terms):
    own, near, far, last = terms
    pair = summed(far, send(last, NEAR)).astype(jnp.bfloat16)
    near, pair = lax.optimization_barrier((near, pair))
    return summed(own, send(near, NEAR), send(pair, FAR))


def shards(
    state, patch_slot, section_active, qkv_weight, out_weight, norm_gain, stale_keys, stale_values
):
    section_count = lax.axis_size("section")
    section_index = lax.axis_index("section")
    w = jnp.transpose(qkv_weight[0], (1, 0, 2))
    wo = out_weight[0]
    w, wo, kc, vc = loaded(w, wo, stale_keys[0], stale_values[0])
    block_count = section_active[0]
    n = lax.axis_size("uly")
    patch_rows = state.shape[1] * n
    own = state[0]
    blocks = gathered(own)
    for tick in range(TICKS):
        slot = patch_slot[(section_index - tick) % section_count]
        for index in range(PASSES):
            applies = block_count > index
            info = jnp.stack([slot * patch_rows, applies.astype(jnp.int32)])
            terms, kc, vc = block_terms(info, blocks, norm_gain, w, wo, kc, vc)
            updated = own.astype(jnp.float32) + scattered(terms)
            updated = jnp.where(applies, updated.astype(jnp.bfloat16), own)
            last = index == PASSES - 1
            if last and tick == TICKS - 1:
                return send(updated, STAY, 1)[None]
            blocks = gathered(updated, 1 if last else 0)
            own = blocks[0]


def solution(mesh):
    return jax.shard_map(
        shards,
        mesh=mesh,
        in_specs=(
            P("section", "uly", None),
            P(),
            P("section"),
            P("section", None, None, "uly"),
            P("section", "uly", None),
            P("section", None),
            P("section", None, "uly"),
            P("section", None, "uly"),
        ),
        out_specs=P("section", "uly", None),
        check_vma=False,
    )
```

```python
import functools
import math

import jax
import jax.numpy as jnp
from jax import lax
from jax.experimental import pallas as pl
from jax.experimental.pallas import tpu as pltpu
from jax.sharding import PartitionSpec as P

HD = 128
TICKS = 3
PASSES = 2
VMEM_LIMIT = 24 * 2**20
SCALE = HD ** (-0.5) * math.log2(math.e)
OUT_STEPS = 3


def block_kernel(chunks, info, *refs):
    blocks = refs[:chunks]
    gain, w, wo, _, _ = refs[chunks:chunks + 5]
    terms = refs[chunks + 5:2 * chunks + 5]
    kc, vc, normed, attended = refs[2 * chunks + 5:]
    rows = blocks[0].shape[0]
    total_rows = rows * chunks
    heads = kc.shape[1] // HD

    @pl.when(info[1] > 0)
    def _():
        gain_row = gain[...].astype(jnp.float32)
        for c in range(chunks):
            wide = blocks[c][...].astype(jnp.float32)
            mean_square = jnp.mean(wide * wide, axis=-1, keepdims=True)
            normed[pl.ds(c * rows, rows), :] = (
                wide * lax.rsqrt(mean_square + 1e-06) * gain_row
            ).astype(jnp.bfloat16)
        projected = jnp.dot(
            normed[...], w[...], preferred_element_type=jnp.float32
        ).astype(jnp.bfloat16)
        width = heads * HD
        start = pl.multiple_of(info[0], total_rows)
        kc[pl.ds(start, total_rows), :] = projected[:, width:2 * width]
        vc[pl.ds(start, total_rows), :] = projected[:, 2 * width:]
        for h in range(heads):
            cols = pl.ds(h * HD, HD)
            scores = lax.dot_general(
                projected[:, h * HD:(h + 1) * HD],
                kc[:, cols],
                (((1,), (1,)), ((), ())),
                preferred_element_type=jnp.float32,
            )
            top = jnp.max(scores, axis=-1, keepdims=True)
            weights = jnp.exp2((scores - top) * SCALE)
            share = 1.0 / jnp.sum(weights, axis=-1, keepdims=True)
            mixed = jnp.dot(
                weights.astype(jnp.bfloat16), vc[:, cols], preferred_element_type=jnp.float32
            )
            attended[:, cols] = (mixed * share).astype(jnp.bfloat16)
        step = wo.shape[1] // OUT_STEPS
        for i in range(OUT_STEPS):
            cols = pl.ds(i * step, step)
            product = jnp.dot(
                attended[...], wo[:, cols], preferred_element_type=jnp.float32
            ).astype(jnp.bfloat16)
            for c in range(chunks):
                terms[c][:, cols] = product[c * rows:(c + 1) * rows]


def load_kernel(w_hbm, wo_hbm, kc_hbm, vc_hbm, w, wo, kc, vc, sems):
    parts, _, width = w_hbm.shape
    pairs = [(w_hbm.at[i], w.at[:, pl.ds(i * width, width)]) for i in range(parts)]
    pairs += [(wo_hbm, wo), (kc_hbm, kc), (vc_hbm, vc)]
    copies = [pltpu.make_async_copy(a, b, sems.at[i]) for i, (a, b) in enumerate(pairs)]
    for copy in copies:
        copy.start()
    for copy in copies:
        copy.wait()


def loaded(w, wo, kc, vc):
    parts, depth, width = w.shape
    arrays = (w, wo, kc, vc)
    shapes = [(depth, parts * width), wo.shape, kc.shape, vc.shape]
    return pl.pallas_call(
        load_kernel,
        out_shape=[pltpu.VMEM(shape, w.dtype) for shape in shapes],
        in_specs=[pl.BlockSpec(memory_space=pl.ANY)] * len(arrays),
        out_specs=[pl.BlockSpec(memory_space=pltpu.VMEM)] * len(arrays),
        scratch_shapes=[pltpu.SemaphoreType.DMA((parts + 3,))],
        compiler_params=pltpu.CompilerParams(vmem_limit_bytes=VMEM_LIMIT),
        cost_estimate=pl.CostEstimate(
            flops=0, bytes_accessed=2 * sum(a.size for a in arrays), transcendentals=0
        ),
    )(*[pltpu.with_memory_space_constraint(a, pltpu.HBM) for a in arrays])


def block_terms(info, blocks, gain, w, wo, kc, vc):
    chunks = len(blocks)
    rows, width = blocks[0].shape
    vmem = pl.BlockSpec(memory_space=pltpu.VMEM)
    row_count = rows * chunks
    flops = 2 * row_count * (w.size + wo.size + 2 * kc.size)
    held = [pltpu.with_memory_space_constraint(x, pltpu.VMEM) for x in (w, wo, kc, vc)]
    cache = pltpu.VMEM(kc.shape, kc.dtype)
    out = pl.pallas_call(
        functools.partial(block_kernel, chunks),
        out_shape=[jax.ShapeDtypeStruct((rows, width), jnp.bfloat16)] * chunks + [cache] * 2,
        in_specs=[pl.BlockSpec(memory_space=pltpu.SMEM)] + [vmem] * (chunks + 5),
        out_specs=[vmem] * (chunks + 2),
        input_output_aliases={chunks + 4: chunks, chunks + 5: chunks + 1},
        scratch_shapes=[
            pltpu.VMEM((row_count, width), jnp.bfloat16),
            pltpu.VMEM((row_count, kc.shape[1]), jnp.bfloat16),
        ],
        compiler_params=pltpu.CompilerParams(vmem_limit_bytes=VMEM_LIMIT),
        cost_estimate=pl.CostEstimate(
            flops=flops, bytes_accessed=2 * (w.size + wo.size), transcendentals=0
        ),
    )(info, *blocks, gain, *held)
    return out[:chunks], out[chunks], out[chunks + 1]


STAY = ((0, 0), (1, 1), (2, 2), (3, 3))
NEAR = ((0, 1), (1, 0), (2, 3), (3, 2))
FAR = ((0, 3), (1, 2), (2, 1), (3, 0))


def send(block, pairs, hop=0):
    sections = lax.axis_size("section")
    n = lax.axis_size("uly")
    route = [
        (s * n + a, (s + hop) % sections * n + b) for s in range(sections) for a, b in pairs
    ]
    return lax.ppermute(block, ("section", "uly"), route)


def summed(*blocks):
    total = blocks[0].astype(jnp.float32)
    for block in blocks[1:]:
        total = total + block.astype(jnp.float32)
    return total


def gathered(own, hop=0, between=lambda far: far):
    far = send(own, FAR, hop)
    near = send(own, NEAR, hop)
    first = send(own, STAY, hop) if hop else own
    far = between(far)
    return [first, near, far, send(far, NEAR)]


def scattered(terms):
    own, near, far, last = terms
    pair = summed(far, send(last, NEAR)).astype(jnp.bfloat16)
    near, pair = lax.optimization_barrier((near, pair))
    return summed(own, send(near, NEAR), send(pair, FAR))


def shards(
    state, patch_slot, section_active, qkv_weight, out_weight, norm_gain, stale_keys, stale_values
):
    section_count = lax.axis_size("section")
    section_index = lax.axis_index("section")
    block_count = section_active[0]
    n = lax.axis_size("uly")
    patch_rows = state.shape[1] * n
    own = state[0]
    stored = (
        jnp.transpose(qkv_weight[0], (1, 0, 2)), out_weight[0], stale_keys[0], stale_values[0]
    )
    held = []

    def load(far):
        far, *rest = lax.optimization_barrier((far, *loaded(*stored)))
        held.extend(rest)
        return far

    blocks = gathered(own, between=load)
    w, wo, kc, vc = held
    for tick in range(TICKS):
        slot = patch_slot[(section_index - tick) % section_count]
        for index in range(PASSES):
            applies = block_count > index
            info = jnp.stack([slot * patch_rows, applies.astype(jnp.int32)])
            terms, kc, vc = block_terms(info, blocks, norm_gain, w, wo, kc, vc)
            updated = own.astype(jnp.float32) + scattered(terms)
            updated = jnp.where(applies, updated.astype(jnp.bfloat16), own)
            last = index == PASSES - 1
            if last and tick == TICKS - 1:
                return send(updated, STAY, 1)[None]
            blocks = gathered(updated, 1 if last else 0)
            own = blocks[0]


def solution(mesh):
    return jax.shard_map(
        shards,
        mesh=mesh,
        in_specs=(
            P("section", "uly", None),
            P(),
            P("section"),
            P("section", None, None, "uly"),
            P("section", "uly", None),
            P("section", None),
            P("section", None, "uly"),
            P("section", None, "uly"),
        ),
        out_specs=P("section", "uly", None),
        check_vma=False,
    )
```

```python
import functools
import math

import jax
import jax.numpy as jnp
from jax import lax
from jax.experimental import pallas as pl
from jax.experimental.pallas import tpu as pltpu
from jax.sharding import PartitionSpec as P

HD = 128
TICKS = 3
PASSES = 2
VMEM_LIMIT = 24 * 2**20
SCALE = HD ** (-0.5) * math.log2(math.e)
OUT_STEPS = 3


def block_kernel(chunks, info, *refs):
    blocks = refs[:chunks]
    gain, w, wo, _, _ = refs[chunks:chunks + 5]
    terms = refs[chunks + 5:2 * chunks + 5]
    kc, vc, normed, attended = refs[2 * chunks + 5:]
    rows = blocks[0].shape[0]
    total_rows = rows * chunks
    heads = kc.shape[1] // HD

    @pl.when(info[1] > 0)
    def _():
        gain_row = gain[...].astype(jnp.float32)
        for c in range(chunks):
            wide = blocks[c][...].astype(jnp.float32)
            mean_square = jnp.mean(wide * wide, axis=-1, keepdims=True)
            normed[pl.ds(c * rows, rows), :] = (
                wide * lax.rsqrt(mean_square + 1e-06) * gain_row
            ).astype(jnp.bfloat16)
        projected = jnp.dot(
            normed[...], w[...], preferred_element_type=jnp.float32
        ).astype(jnp.bfloat16)
        width = heads * HD
        start = pl.multiple_of(info[0], total_rows)
        kc[pl.ds(start, total_rows), :] = projected[:, width:2 * width]
        vc[pl.ds(start, total_rows), :] = projected[:, 2 * width:]
        for h in range(heads):
            cols = pl.ds(h * HD, HD)
            scores = lax.dot_general(
                projected[:, h * HD:(h + 1) * HD],
                kc[:, cols],
                (((1,), (1,)), ((), ())),
                preferred_element_type=jnp.float32,
            )
            top = jnp.max(scores, axis=-1, keepdims=True)
            weights = jnp.exp2((scores - top) * SCALE)
            share = 1.0 / jnp.sum(weights, axis=-1, keepdims=True)
            mixed = jnp.dot(
                weights.astype(jnp.bfloat16), vc[:, cols], preferred_element_type=jnp.float32
            )
            attended[:, cols] = (mixed * share).astype(jnp.bfloat16)
        step = wo.shape[1] // OUT_STEPS
        for i in range(OUT_STEPS):
            cols = pl.ds(i * step, step)
            product = jnp.dot(
                attended[...], wo[:, cols], preferred_element_type=jnp.float32
            ).astype(jnp.bfloat16)
            for c in range(chunks):
                terms[c][:, cols] = product[c * rows:(c + 1) * rows]


def load_kernel(w_hbm, wo_hbm, kc_hbm, vc_hbm, gain_hbm, w, wo, kc, vc, gain, sems):
    parts, _, width = w_hbm.shape
    pairs = [(w_hbm.at[i], w.at[:, pl.ds(i * width, width)]) for i in range(parts)]
    pairs += [(wo_hbm, wo), (kc_hbm, kc), (vc_hbm, vc), (gain_hbm, gain)]
    copies = [pltpu.make_async_copy(a, b, sems.at[i]) for i, (a, b) in enumerate(pairs)]
    for copy in copies:
        copy.start()
    for copy in copies:
        copy.wait()


def loaded(w, wo, kc, vc, gain):
    parts, depth, width = w.shape
    arrays = (w, wo, kc, vc, gain)
    shapes = [(depth, parts * width)] + [a.shape for a in arrays[1:]]
    return pl.pallas_call(
        load_kernel,
        out_shape=[pltpu.VMEM(shape, w.dtype) for shape in shapes],
        in_specs=[pl.BlockSpec(memory_space=pl.ANY)] * len(arrays),
        out_specs=[pl.BlockSpec(memory_space=pltpu.VMEM)] * len(arrays),
        scratch_shapes=[pltpu.SemaphoreType.DMA((parts + 4,))],
        compiler_params=pltpu.CompilerParams(vmem_limit_bytes=VMEM_LIMIT),
        cost_estimate=pl.CostEstimate(
            flops=0, bytes_accessed=2 * sum(a.size for a in arrays), transcendentals=0
        ),
    )(*[pltpu.with_memory_space_constraint(a, pltpu.HBM) for a in arrays])


def block_terms(info, blocks, gain, w, wo, kc, vc):
    chunks = len(blocks)
    rows, width = blocks[0].shape
    vmem = pl.BlockSpec(memory_space=pltpu.VMEM)
    row_count = rows * chunks
    flops = 2 * row_count * (w.size + wo.size + 2 * kc.size)
    held = [pltpu.with_memory_space_constraint(x, pltpu.VMEM) for x in (gain, w, wo, kc, vc)]
    cache = pltpu.VMEM(kc.shape, kc.dtype)
    out = pl.pallas_call(
        functools.partial(block_kernel, chunks),
        out_shape=[jax.ShapeDtypeStruct((rows, width), jnp.bfloat16)] * chunks + [cache] * 2,
        in_specs=[pl.BlockSpec(memory_space=pltpu.SMEM)] + [vmem] * (chunks + 5),
        out_specs=[vmem] * (chunks + 2),
        input_output_aliases={chunks + 4: chunks, chunks + 5: chunks + 1},
        scratch_shapes=[
            pltpu.VMEM((row_count, width), jnp.bfloat16),
            pltpu.VMEM((row_count, kc.shape[1]), jnp.bfloat16),
        ],
        compiler_params=pltpu.CompilerParams(vmem_limit_bytes=VMEM_LIMIT),
        cost_estimate=pl.CostEstimate(
            flops=flops, bytes_accessed=2 * (w.size + wo.size), transcendentals=0
        ),
    )(info, *blocks, *held)
    return out[:chunks], out[chunks], out[chunks + 1]


STAY = ((0, 0), (1, 1), (2, 2), (3, 3))
NEAR = ((0, 1), (1, 0), (2, 3), (3, 2))
FAR = ((0, 2), (1, 3), (2, 0), (3, 1))


def send(block, pairs, hop=0):
    sections = lax.axis_size("section")
    n = lax.axis_size("uly")
    route = [
        (s * n + a, (s + hop) % sections * n + b) for s in range(sections) for a, b in pairs
    ]
    return lax.ppermute(block, ("section", "uly"), route)


def summed(*blocks):
    total = blocks[0].astype(jnp.float32)
    for block in blocks[1:]:
        total = total + block.astype(jnp.float32)
    return total


def gathered(own, hop=0, between=lambda far: far):
    far = send(own, FAR, hop)
    near = send(own, NEAR, hop)
    first = send(own, STAY, hop) if hop else own
    far = between(far)
    return [first, near, far, send(far, NEAR)]


def scattered(terms):
    own, near, far, last = terms
    pair = summed(far, send(last, NEAR)).astype(jnp.bfloat16)
    near, pair = lax.optimization_barrier((near, pair))
    far = send(pair, FAR)
    near = send(near, NEAR)
    return lax.optimization_barrier(summed(own, far)) + near.astype(jnp.float32)


def shards(
    state, patch_slot, section_active, qkv_weight, out_weight, norm_gain, stale_keys, stale_values
):
    section_count = lax.axis_size("section")
    section_index = lax.axis_index("section")
    block_count = section_active[0]
    n = lax.axis_size("uly")
    patch_rows = state.shape[1] * n
    own = state[0]
    stored = (
        jnp.transpose(qkv_weight[0], (1, 0, 2)),
        out_weight[0],
        stale_keys[0],
        stale_values[0],
        norm_gain,
    )
    held = []

    def load(far):
        far, *rest = lax.optimization_barrier((far, *loaded(*stored)))
        held.extend(rest)
        return far

    blocks = gathered(own, between=load)
    w, wo, kc, vc, gain = held
    for tick in range(TICKS):
        slot = patch_slot[(section_index - tick) % section_count]
        for index in range(PASSES):
            applies = block_count > index
            info = jnp.stack([slot * patch_rows, applies.astype(jnp.int32)])
            terms, kc, vc = block_terms(info, blocks, gain, w, wo, kc, vc)
            updated = own.astype(jnp.float32) + scattered(terms)
            updated = jnp.where(applies, updated.astype(jnp.bfloat16), own)
            last = index == PASSES - 1
            if last and tick == TICKS - 1:
                return send(updated, STAY, 1)[None]
            blocks = gathered(updated, 1 if last else 0)
            own = blocks[0]


def solution(mesh):
    return jax.shard_map(
        shards,
        mesh=mesh,
        in_specs=(
            P("section", "uly", None),
            P(),
            P("section"),
            P("section", None, None, "uly"),
            P("section", "uly", None),
            P("section", None),
            P("section", None, "uly"),
            P("section", None, "uly"),
        ),
        out_specs=P("section", "uly", None),
        check_vma=False,
    )
```

```python
import functools
import math

import jax
import jax.numpy as jnp
from jax import lax
from jax.experimental import pallas as pl
from jax.experimental.pallas import tpu as pltpu
from jax.sharding import PartitionSpec as P

HD = 128
TICKS = 3
PASSES = 2
VMEM_LIMIT = 12 * 2**20
SCALE = HD ** (-0.5) * math.log2(math.e)
OUT_STEPS = 3


def block_kernel(chunks, info, *refs):
    blocks = refs[:chunks]
    gain, w, wo, _, _ = refs[chunks:chunks + 5]
    terms = refs[chunks + 5:2 * chunks + 5]
    kc, vc, normed, attended = refs[2 * chunks + 5:]
    rows = blocks[0].shape[0]
    total_rows = rows * chunks
    heads = kc.shape[1] // HD

    @pl.when(info[1] > 0)
    def _():
        gain_row = gain[...].astype(jnp.float32)
        for c in range(chunks):
            wide = blocks[c][...].astype(jnp.float32)
            mean_square = jnp.mean(wide * wide, axis=-1, keepdims=True)
            normed[pl.ds(c * rows, rows), :] = (
                wide * lax.rsqrt(mean_square + 1e-06) * gain_row
            ).astype(jnp.bfloat16)
        projected = jnp.dot(
            normed[...], w[...], preferred_element_type=jnp.float32
        ).astype(jnp.bfloat16)
        width = heads * HD
        start = pl.multiple_of(info[0], total_rows)
        kc[pl.ds(start, total_rows), :] = projected[:, width:2 * width]
        vc[pl.ds(start, total_rows), :] = projected[:, 2 * width:]
        for h in range(heads):
            cols = pl.ds(h * HD, HD)
            scores = lax.dot_general(
                projected[:, h * HD:(h + 1) * HD],
                kc[:, cols],
                (((1,), (1,)), ((), ())),
                preferred_element_type=jnp.float32,
            )
            top = jnp.max(scores, axis=-1, keepdims=True)
            weights = jnp.exp2((scores - top) * SCALE)
            share = 1.0 / jnp.sum(weights, axis=-1, keepdims=True)
            mixed = jnp.dot(
                weights.astype(jnp.bfloat16), vc[:, cols], preferred_element_type=jnp.float32
            )
            attended[:, cols] = (mixed * share).astype(jnp.bfloat16)
        step = wo.shape[1] // OUT_STEPS
        for i in range(OUT_STEPS):
            cols = pl.ds(i * step, step)
            product = jnp.dot(
                attended[...], wo[:, cols], preferred_element_type=jnp.float32
            ).astype(jnp.bfloat16)
            for c in range(chunks):
                terms[c][:, cols] = product[c * rows:(c + 1) * rows]


def load_kernel(w_hbm, wo_hbm, kc_hbm, vc_hbm, gain_hbm, w, wo, kc, vc, gain, sems):
    parts, _, width = w_hbm.shape
    pairs = [(w_hbm.at[i], w.at[:, pl.ds(i * width, width)]) for i in range(parts)]
    pairs += [(wo_hbm, wo), (kc_hbm, kc), (vc_hbm, vc), (gain_hbm, gain)]
    copies = [pltpu.make_async_copy(a, b, sems.at[i]) for i, (a, b) in enumerate(pairs)]
    for copy in copies:
        copy.start()
    for copy in copies:
        copy.wait()


def loaded(w, wo, kc, vc, gain):
    parts, depth, width = w.shape
    arrays = (w, wo, kc, vc, gain)
    shapes = [(depth, parts * width)] + [a.shape for a in arrays[1:]]
    return pl.pallas_call(
        load_kernel,
        out_shape=[pltpu.VMEM(shape, w.dtype) for shape in shapes],
        in_specs=[pl.BlockSpec(memory_space=pl.ANY)] * len(arrays),
        out_specs=[pl.BlockSpec(memory_space=pltpu.VMEM)] * len(arrays),
        scratch_shapes=[pltpu.SemaphoreType.DMA((parts + 4,))],
        compiler_params=pltpu.CompilerParams(vmem_limit_bytes=VMEM_LIMIT),
        cost_estimate=pl.CostEstimate(
            flops=0, bytes_accessed=2 * sum(a.size for a in arrays), transcendentals=0
        ),
    )(*[pltpu.with_memory_space_constraint(a, pltpu.HBM) for a in arrays])


def block_terms(info, blocks, gain, w, wo, kc, vc):
    chunks = len(blocks)
    rows, width = blocks[0].shape
    vmem = pl.BlockSpec(memory_space=pltpu.VMEM)
    row_count = rows * chunks
    flops = 2 * row_count * (w.size + wo.size + 2 * kc.size)
    held = [pltpu.with_memory_space_constraint(x, pltpu.VMEM) for x in (gain, w, wo, kc, vc)]
    cache = pltpu.VMEM(kc.shape, kc.dtype)
    out = pl.pallas_call(
        functools.partial(block_kernel, chunks),
        out_shape=[jax.ShapeDtypeStruct((rows, width), jnp.bfloat16)] * chunks + [cache] * 2,
        in_specs=[pl.BlockSpec(memory_space=pltpu.SMEM)] + [vmem] * (chunks + 5),
        out_specs=[vmem] * (chunks + 2),
        input_output_aliases={chunks + 4: chunks, chunks + 5: chunks + 1},
        scratch_shapes=[
            pltpu.VMEM((row_count, width), jnp.bfloat16),
            pltpu.VMEM((row_count, kc.shape[1]), jnp.bfloat16),
        ],
        compiler_params=pltpu.CompilerParams(vmem_limit_bytes=VMEM_LIMIT),
        cost_estimate=pl.CostEstimate(
            flops=flops, bytes_accessed=2 * (w.size + wo.size), transcendentals=0
        ),
    )(info, *blocks, *held)
    return out[:chunks], out[chunks], out[chunks + 1]


STAY = ((0, 0), (1, 1), (2, 2), (3, 3))
NEAR = ((0, 1), (1, 0), (2, 3), (3, 2))
FAR = ((0, 3), (1, 2), (2, 1), (3, 0))


def send(block, pairs, hop=0):
    sections = lax.axis_size("section")
    n = lax.axis_size("uly")
    route = [
        (s * n + a, (s + hop) % sections * n + b) for s in range(sections) for a, b in pairs
    ]
    return lax.ppermute(block, ("section", "uly"), route)


def summed(*blocks):
    total = blocks[0].astype(jnp.float32)
    for block in blocks[1:]:
        total = total + block.astype(jnp.float32)
    return total


def gathered(own, hop=0):
    far = send(own, FAR, hop)
    near = send(own, NEAR, hop)
    first = send(own, STAY, hop) if hop else own
    return [first, near, far, send(far, NEAR)]


def scattered(terms):
    own, near, far, last = terms
    pair = summed(far, send(last, NEAR)).astype(jnp.bfloat16)
    near, pair = lax.optimization_barrier((near, pair))
    far = send(pair, FAR)
    near = send(near, NEAR)
    return lax.optimization_barrier(summed(own, far)) + near.astype(jnp.float32)


def shards(
    state, patch_slot, section_active, qkv_weight, out_weight, norm_gain, stale_keys, stale_values
):
    section_count = lax.axis_size("section")
    section_index = lax.axis_index("section")
    block_count = section_active[0]
    n = lax.axis_size("uly")
    patch_rows = state.shape[1] * n
    own = state[0]
    stored = (
        jnp.transpose(qkv_weight[0], (1, 0, 2)),
        out_weight[0],
        stale_keys[0],
        stale_values[0],
        norm_gain,
    )
    w, wo, kc, vc, gain = loaded(*stored)
    blocks = gathered(own)
    for tick in range(TICKS):
        slot = patch_slot[(section_index - tick) % section_count]
        for index in range(PASSES):
            applies = block_count > index
            info = jnp.stack([slot * patch_rows, applies.astype(jnp.int32)])
            terms, kc, vc = block_terms(info, blocks, gain, w, wo, kc, vc)
            updated = own.astype(jnp.float32) + scattered(terms)
            updated = jnp.where(applies, updated.astype(jnp.bfloat16), own)
            last = index == PASSES - 1
            if last and tick == TICKS - 1:
                return send(updated, STAY, 1)[None]
            blocks = gathered(updated, 1 if last else 0)
            own = blocks[0]


def solution(mesh):
    return jax.shard_map(
        shards,
        mesh=mesh,
        in_specs=(
            P("section", "uly", None),
            P(),
            P("section"),
            P("section", None, None, "uly"),
            P("section", "uly", None),
            P("section", None),
            P("section", None, "uly"),
            P("section", None, "uly"),
        ),
        out_specs=P("section", "uly", None),
        check_vma=False,
    )
```

```python
import functools
import math

import jax
import jax.numpy as jnp
from jax import lax
from jax.experimental import pallas as pl
from jax.experimental.pallas import tpu as pltpu
from jax.sharding import PartitionSpec as P

HD = 128
TICKS = 3
PASSES = 2
VMEM_LIMIT = 12 * 2**20
SCALE = HD ** (-0.5) * math.log2(math.e)
OUT_STEPS = 3
SHARES = (1, 1)


def row_spans(refs):
    start = 0
    for ref in refs:
        yield start, start + ref.shape[0], ref
        start += ref.shape[0]


def block_kernel(in_count, out_count, info, *refs):
    blocks = refs[:in_count]
    gain, w, wo, _, _ = refs[in_count:in_count + 5]
    terms = refs[in_count + 5:in_count + 5 + out_count]
    kc, vc, normed, attended = refs[in_count + 5 + out_count:]
    total_rows = normed.shape[0]
    heads = kc.shape[1] // HD

    @pl.when(info[1] > 0)
    def _():
        gain_row = gain[...].astype(jnp.float32)
        for first, end, block in row_spans(blocks):
            wide = block[...].astype(jnp.float32)
            mean_square = jnp.mean(wide * wide, axis=-1, keepdims=True)
            normed[first:end, :] = (
                wide * lax.rsqrt(mean_square + 1e-06) * gain_row
            ).astype(jnp.bfloat16)
        projected = jnp.dot(
            normed[...], w[...], preferred_element_type=jnp.float32
        ).astype(jnp.bfloat16)
        width = heads * HD
        start = pl.multiple_of(info[0], total_rows)
        kc[pl.ds(start, total_rows), :] = projected[:, width:2 * width]
        vc[pl.ds(start, total_rows), :] = projected[:, 2 * width:]
        for h in range(heads):
            cols = pl.ds(h * HD, HD)
            scores = lax.dot_general(
                projected[:, h * HD:(h + 1) * HD],
                kc[:, cols],
                (((1,), (1,)), ((), ())),
                preferred_element_type=jnp.float32,
            )
            top = jnp.max(scores, axis=-1, keepdims=True)
            weights = jnp.exp2((scores - top) * SCALE)
            share = 1.0 / jnp.sum(weights, axis=-1, keepdims=True)
            mixed = jnp.dot(
                weights.astype(jnp.bfloat16), vc[:, cols], preferred_element_type=jnp.float32
            )
            attended[:, cols] = (mixed * share).astype(jnp.bfloat16)
        step = wo.shape[1] // OUT_STEPS
        for i in range(OUT_STEPS):
            cols = pl.ds(i * step, step)
            product = jnp.dot(
                attended[...], wo[:, cols], preferred_element_type=jnp.float32
            ).astype(jnp.bfloat16)
            for first, end, term in row_spans(terms):
                term[:, cols] = product[first:end]

    @pl.when(info[1] <= 0)
    def _():
        for term in terms:
            term[...] = jnp.zeros_like(term)


def load_kernel(w_hbm, wo_hbm, kc_hbm, vc_hbm, gain_hbm, w, wo, kc, vc, gain, sems):
    parts, _, width = w_hbm.shape
    pairs = [(w_hbm.at[i], w.at[:, pl.ds(i * width, width)]) for i in range(parts)]
    pairs += [(wo_hbm, wo), (kc_hbm, kc), (vc_hbm, vc), (gain_hbm, gain)]
    copies = [pltpu.make_async_copy(a, b, sems.at[i]) for i, (a, b) in enumerate(pairs)]
    for copy in copies:
        copy.start()
    for copy in copies:
        copy.wait()


def loaded(w, wo, kc, vc, gain):
    parts, depth, width = w.shape
    arrays = (w, wo, kc, vc, gain)
    shapes = [(depth, parts * width)] + [a.shape for a in arrays[1:]]
    return pl.pallas_call(
        load_kernel,
        out_shape=[pltpu.VMEM(shape, w.dtype) for shape in shapes],
        in_specs=[pl.BlockSpec(memory_space=pl.ANY)] * len(arrays),
        out_specs=[pl.BlockSpec(memory_space=pltpu.VMEM)] * len(arrays),
        scratch_shapes=[pltpu.SemaphoreType.DMA((parts + 4,))],
        compiler_params=pltpu.CompilerParams(vmem_limit_bytes=VMEM_LIMIT),
        cost_estimate=pl.CostEstimate(
            flops=0, bytes_accessed=2 * sum(a.size for a in arrays), transcendentals=0
        ),
    )(*[pltpu.with_memory_space_constraint(a, pltpu.HBM) for a in arrays])


def block_terms(info, blocks, rows_out, gain, w, wo, kc, vc):
    count, width = len(blocks), blocks[0].shape[1]
    row_count = sum(rows_out)
    vmem = pl.BlockSpec(memory_space=pltpu.VMEM)
    flops = 2 * row_count * (w.size + wo.size + 2 * kc.size)
    held = [pltpu.with_memory_space_constraint(x, pltpu.VMEM) for x in (gain, w, wo, kc, vc)]
    cache = pltpu.VMEM(kc.shape, kc.dtype)
    out = pl.pallas_call(
        functools.partial(block_kernel, count, len(rows_out)),
        out_shape=[jax.ShapeDtypeStruct((rows, width), jnp.bfloat16) for rows in rows_out]
        + [cache] * 2,
        in_specs=[pl.BlockSpec(memory_space=pltpu.SMEM)] + [vmem] * (count + 5),
        out_specs=[vmem] * (len(rows_out) + 2),
        input_output_aliases={count + 4: len(rows_out), count + 5: len(rows_out) + 1},
        scratch_shapes=[
            pltpu.VMEM((row_count, width), jnp.bfloat16),
            pltpu.VMEM((row_count, kc.shape[1]), jnp.bfloat16),
        ],
        compiler_params=pltpu.CompilerParams(vmem_limit_bytes=VMEM_LIMIT),
        cost_estimate=pl.CostEstimate(
            flops=flops, bytes_accessed=2 * (w.size + wo.size), transcendentals=0
        ),
    )(info, *blocks, *held)
    return out[:-2], out[-2], out[-1]


STAY = ((0, 0), (1, 1), (2, 2), (3, 3))
NEAR = ((0, 1), (1, 0), (2, 3), (3, 2))
FAR = ((0, 3), (1, 2), (2, 1), (3, 0))


def send(block, pairs, hop=0):
    sections = lax.axis_size("section")
    n = lax.axis_size("uly")
    route = [
        (s * n + a, (s + hop) % sections * n + b) for s in range(sections) for a, b in pairs
    ]
    return lax.ppermute(block, ("section", "uly"), route)


def summed(*blocks):
    total = blocks[0].astype(jnp.float32)
    for block in blocks[1:]:
        total = total + block.astype(jnp.float32)
    return total


def summed(*blocks):
    total = blocks[0].astype(jnp.float32)
    for block in blocks[1:]:
        total = total + block.astype(jnp.float32)
    return total


def rounded(*blocks):
    return summed(*blocks).astype(jnp.bfloat16)


def behind(block, other):
    return lax.optimization_barrier((block, other))[0]


def pieces_of(rows):
    return [rows * share // sum(SHARES) for share in SHARES]


def cut(blocks, sizes):
    whole = jnp.concatenate(blocks)
    starts = [sum(sizes[:i]) for i in range(len(sizes))]
    return [whole[start:start + size] for start, size in zip(starts, sizes)]


def gathered(own, low):
    far = send(own, FAR)
    near = send(own, NEAR)
    last = send(far, NEAR)
    kept = [jnp.where(low, own, far), jnp.where(low, far, own)]
    return kept, [jnp.where(low, near, last), jnp.where(low, last, near)]


def passed_on(kept, terms, hop):
    count = len(kept)
    next_kept, next_others = [], []
    pair = None
    for current, mine, partners in zip(kept, terms[:count], terms[count:]):
        partners = partners if pair is None else behind(partners, pair)
        pair = rounded(mine, send(partners, NEAR))
        updated = rounded(current, pair, send(pair, FAR))
        next_others.append(send(updated, NEAR, hop))
        next_kept.append(send(updated, STAY, hop) if hop else updated)
    return next_kept, next_others


def delivered(kept, terms, low):
    first, second, near_first, near_second = terms
    last = send(jnp.where(low, near_second, near_first), NEAR)
    before = jnp.where(low, *cut(kept, [first.shape[0], second.shape[0]]))
    base = send(rounded(before, jnp.where(low, first, second)), STAY, 1)
    pair = rounded(jnp.where(low, second, first), last)
    near, pair = lax.optimization_barrier((jnp.where(low, near_first, near_second), pair))
    far = send(pair, FAR, 1)
    near = send(near, NEAR, 1)
    return rounded(base, far, near)


def shards(
    state, patch_slot, section_active, qkv_weight, out_weight, norm_gain, stale_keys, stale_values
):
    section_count = lax.axis_size("section")
    section_index = lax.axis_index("section")
    block_count = section_active[0]
    n = lax.axis_size("uly")
    low = lax.axis_index("uly") < n // 2
    shard_rows = state.shape[1]
    patch_rows = shard_rows * n
    stored = (
        jnp.transpose(qkv_weight[0], (1, 0, 2)),
        out_weight[0],
        stale_keys[0],
        stale_values[0],
        norm_gain,
    )
    w, wo, kc, vc, gain = loaded(*stored)
    kept, others = gathered(state[0], low)
    sizes = pieces_of(patch_rows // 2)
    for tick in range(TICKS):
        slot = patch_slot[(section_index - tick) % section_count]
        for index in range(PASSES):
            applies = block_count > index
            info = jnp.stack([slot * patch_rows, applies.astype(jnp.int32)])
            last = index == PASSES - 1
            final = last and tick == TICKS - 1
            rows_out = [shard_rows] * n if final else sizes * 2
            terms, kc, vc = block_terms(info, kept + others, rows_out, gain, w, wo, kc, vc)
            if final:
                return delivered(kept, terms, low)[None]
            kept = cut(kept, sizes) if tick + index == 0 else kept
            kept, others = passed_on(kept, terms, 1 if last else 0)


def solution(mesh):
    return jax.shard_map(
        shards,
        mesh=mesh,
        in_specs=(
            P("section", "uly", None),
            P(),
            P("section"),
            P("section", None, None, "uly"),
            P("section", "uly", None),
            P("section", None),
            P("section", None, "uly"),
            P("section", None, "uly"),
        ),
        out_specs=P("section", "uly", None),
        check_vma=False,
    )
```

```python
import functools
import math

import jax
import jax.numpy as jnp
from jax import lax
from jax.experimental import pallas as pl
from jax.experimental.pallas import tpu as pltpu
from jax.sharding import PartitionSpec as P

HD = 128
TICKS = 3
PASSES = 2
VMEM_LIMIT = 12 * 2**20
SCALE = HD ** (-0.5) * math.log2(math.e)
OUT_STEPS = 3
SHARES = (1, 1)


def row_spans(refs):
    start = 0
    for ref in refs:
        yield start, start + ref.shape[0], ref
        start += ref.shape[0]


def block_kernel(in_count, out_count, info, *refs):
    blocks = refs[:in_count]
    gain, w, wo, _, _ = refs[in_count:in_count + 5]
    terms = refs[in_count + 5:in_count + 5 + out_count]
    kc, vc, normed, attended = refs[in_count + 5 + out_count:]
    total_rows = normed.shape[0]
    heads = kc.shape[1] // HD

    @pl.when(info[1] > 0)
    def _():
        gain_row = gain[...].astype(jnp.float32)
        for first, end, block in row_spans(blocks):
            wide = block[...].astype(jnp.float32)
            mean_square = jnp.mean(wide * wide, axis=-1, keepdims=True)
            normed[first:end, :] = (
                wide * lax.rsqrt(mean_square + 1e-06) * gain_row
            ).astype(jnp.bfloat16)
        projected = jnp.dot(
            normed[...], w[...], preferred_element_type=jnp.float32
        ).astype(jnp.bfloat16)
        width = heads * HD
        start = pl.multiple_of(info[0], total_rows)
        kc[pl.ds(start, total_rows), :] = projected[:, width:2 * width]
        vc[pl.ds(start, total_rows), :] = projected[:, 2 * width:]
        for h in range(heads):
            cols = pl.ds(h * HD, HD)
            scores = lax.dot_general(
                projected[:, h * HD:(h + 1) * HD],
                kc[:, cols],
                (((1,), (1,)), ((), ())),
                preferred_element_type=jnp.float32,
            )
            top = jnp.max(scores, axis=-1, keepdims=True)
            weights = jnp.exp2((scores - top) * SCALE)
            share = 1.0 / jnp.sum(weights, axis=-1, keepdims=True)
            mixed = jnp.dot(
                weights.astype(jnp.bfloat16), vc[:, cols], preferred_element_type=jnp.float32
            )
            attended[:, cols] = (mixed * share).astype(jnp.bfloat16)
        step = wo.shape[1] // OUT_STEPS
        for i in range(OUT_STEPS):
            cols = pl.ds(i * step, step)
            product = jnp.dot(
                attended[...], wo[:, cols], preferred_element_type=jnp.float32
            ).astype(jnp.bfloat16)
            for first, end, term in row_spans(terms):
                term[:, cols] = product[first:end]

    @pl.when(info[1] <= 0)
    def _():
        for term in terms:
            term[...] = jnp.zeros_like(term)


def load_kernel(w_hbm, wo_hbm, kc_hbm, vc_hbm, gain_hbm, w, wo, kc, vc, gain, sems):
    parts, _, width = w_hbm.shape
    pairs = [(w_hbm.at[i], w.at[:, pl.ds(i * width, width)]) for i in range(parts)]
    pairs += [(wo_hbm, wo), (kc_hbm, kc), (vc_hbm, vc), (gain_hbm, gain)]
    copies = [pltpu.make_async_copy(a, b, sems.at[i]) for i, (a, b) in enumerate(pairs)]
    for copy in copies:
        copy.start()
    for copy in copies:
        copy.wait()


def loaded(w, wo, kc, vc, gain):
    parts, depth, width = w.shape
    arrays = (w, wo, kc, vc, gain)
    shapes = [(depth, parts * width)] + [a.shape for a in arrays[1:]]
    return pl.pallas_call(
        load_kernel,
        out_shape=[pltpu.VMEM(shape, w.dtype) for shape in shapes],
        in_specs=[pl.BlockSpec(memory_space=pl.ANY)] * len(arrays),
        out_specs=[pl.BlockSpec(memory_space=pltpu.VMEM)] * len(arrays),
        scratch_shapes=[pltpu.SemaphoreType.DMA((parts + 4,))],
        compiler_params=pltpu.CompilerParams(vmem_limit_bytes=VMEM_LIMIT),
        cost_estimate=pl.CostEstimate(
            flops=0, bytes_accessed=2 * sum(a.size for a in arrays), transcendentals=0
        ),
    )(*[pltpu.with_memory_space_constraint(a, pltpu.HBM) for a in arrays])


def block_terms(info, blocks, rows_out, gain, w, wo, kc, vc):
    count, width = len(blocks), blocks[0].shape[1]
    row_count = sum(rows_out)
    vmem = pl.BlockSpec(memory_space=pltpu.VMEM)
    flops = 2 * row_count * (w.size + wo.size + 2 * kc.size)
    held = [pltpu.with_memory_space_constraint(x, pltpu.VMEM) for x in (gain, w, wo, kc, vc)]
    cache = pltpu.VMEM(kc.shape, kc.dtype)
    out = pl.pallas_call(
        functools.partial(block_kernel, count, len(rows_out)),
        out_shape=[jax.ShapeDtypeStruct((rows, width), jnp.bfloat16) for rows in rows_out]
        + [cache] * 2,
        in_specs=[pl.BlockSpec(memory_space=pltpu.SMEM)] + [vmem] * (count + 5),
        out_specs=[vmem] * (len(rows_out) + 2),
        input_output_aliases={count + 4: len(rows_out), count + 5: len(rows_out) + 1},
        scratch_shapes=[
            pltpu.VMEM((row_count, width), jnp.bfloat16),
            pltpu.VMEM((row_count, kc.shape[1]), jnp.bfloat16),
        ],
        compiler_params=pltpu.CompilerParams(vmem_limit_bytes=VMEM_LIMIT),
        cost_estimate=pl.CostEstimate(
            flops=flops, bytes_accessed=2 * (w.size + wo.size), transcendentals=0
        ),
    )(info, *blocks, *held)
    return out[:-2], out[-2], out[-1]


STAY = ((0, 0), (1, 1), (2, 2), (3, 3))
NEAR = ((0, 1), (1, 0), (2, 3), (3, 2))
FAR = ((0, 3), (1, 2), (2, 1), (3, 0))


def send(block, pairs, hop=0):
    sections = lax.axis_size("section")
    n = lax.axis_size("uly")
    route = [
        (s * n + a, (s + hop) % sections * n + b) for s in range(sections) for a, b in pairs
    ]
    return lax.ppermute(block, ("section", "uly"), route)


def summed(*blocks):
    total = blocks[0].astype(jnp.float32)
    for block in blocks[1:]:
        total = total + block.astype(jnp.float32)
    return total


def summed(*blocks):
    total = blocks[0].astype(jnp.float32)
    for block in blocks[1:]:
        total = total + block.astype(jnp.float32)
    return total


def rounded(*blocks):
    return summed(*blocks).astype(jnp.bfloat16)


def behind(block, other):
    return lax.optimization_barrier((block, other))[0]


def pieces_of(rows):
    return [rows * share // sum(SHARES) for share in SHARES]


def cut(blocks, sizes):
    whole = jnp.concatenate(blocks)
    starts = [sum(sizes[:i]) for i in range(len(sizes))]
    return [whole[start:start + size] for start, size in zip(starts, sizes)]


def gathered(own, low):
    far = send(own, FAR)
    near = send(own, NEAR)
    last = send(far, NEAR)
    kept = [jnp.where(low, own, far), jnp.where(low, far, own)]
    return kept, [jnp.where(low, near, last), jnp.where(low, last, near)]


def passed_on(kept, terms, low, hop):
    count = len(kept)
    updated = []
    arrived = send(terms[count], NEAR)
    for i in range(count):
        pair = summed(terms[i], arrived)
        if hop:
            current = jnp.where(low, kept[i], jnp.zeros_like(kept[i]))
            pair = pair + current.astype(jnp.float32)
        pair = pair.astype(jnp.bfloat16)
        if i + 1 < count:
            arrived = send(behind(terms[count + i + 1], pair), NEAR)
        if hop:
            stay = send(pair, STAY, hop)
            updated.append(rounded(stay, send(pair, FAR, hop)))
        else:
            updated.append(rounded(kept[i], pair, send(pair, FAR)))
    return updated, [send(block, NEAR) for block in updated]


def delivered(kept, terms, low):
    first, second, near_first, near_second = terms
    last = send(jnp.where(low, near_second, near_first), NEAR)
    before = jnp.where(low, *cut(kept, [first.shape[0], second.shape[0]]))
    base = send(rounded(before, jnp.where(low, first, second)), STAY, 1)
    pair = rounded(jnp.where(low, second, first), last)
    near, pair = lax.optimization_barrier((jnp.where(low, near_first, near_second), pair))
    far = send(pair, FAR, 1)
    near = send(near, NEAR, 1)
    total = lax.optimization_barrier(summed(base))
    total = lax.optimization_barrier(total + far.astype(jnp.float32))
    return (total + near.astype(jnp.float32)).astype(jnp.bfloat16)


def shards(
    state, patch_slot, section_active, qkv_weight, out_weight, norm_gain, stale_keys, stale_values
):
    section_count = lax.axis_size("section")
    section_index = lax.axis_index("section")
    block_count = section_active[0]
    n = lax.axis_size("uly")
    low = lax.axis_index("uly") < n // 2
    shard_rows = state.shape[1]
    patch_rows = shard_rows * n
    stored = (
        jnp.transpose(qkv_weight[0], (1, 0, 2)),
        out_weight[0],
        stale_keys[0],
        stale_values[0],
        norm_gain,
    )
    w, wo, kc, vc, gain = loaded(*stored)
    kept, others = gathered(state[0], low)
    sizes = pieces_of(patch_rows // 2)
    for tick in range(TICKS):
        slot = patch_slot[(section_index - tick) % section_count]
        for index in range(PASSES):
            applies = block_count > index
            info = jnp.stack([slot * patch_rows, applies.astype(jnp.int32)])
            last = index == PASSES - 1
            final = last and tick == TICKS - 1
            rows_out = [shard_rows] * n if final else sizes * 2
            terms, kc, vc = block_terms(info, kept + others, rows_out, gain, w, wo, kc, vc)
            if final:
                return delivered(kept, terms, low)[None]
            kept = cut(kept, sizes) if tick + index == 0 else kept
            kept, others = passed_on(kept, terms, low, 1 if last else 0)


def solution(mesh):
    return jax.shard_map(
        shards,
        mesh=mesh,
        in_specs=(
            P("section", "uly", None),
            P(),
            P("section"),
            P("section", None, None, "uly"),
            P("section", "uly", None),
            P("section", None),
            P("section", None, "uly"),
            P("section", None, "uly"),
        ),
        out_specs=P("section", "uly", None),
        check_vma=False,
    )
```

```python
import functools
import math

import jax
import jax.numpy as jnp
from jax import lax
from jax.experimental import pallas as pl
from jax.experimental.pallas import tpu as pltpu
from jax.sharding import PartitionSpec as P

HD = 128
TICKS = 3
PASSES = 2
VMEM_LIMIT = 12 * 2**20
SCALE = HD ** (-0.5) * math.log2(math.e)
OUT_STEPS = 3
SHARES = (1, 2, 1)


def row_spans(refs):
    start = 0
    for ref in refs:
        yield start, start + ref.shape[0], ref
        start += ref.shape[0]


def block_kernel(in_count, out_count, info, *refs):
    blocks = refs[:in_count]
    gain, w, wo, _, _ = refs[in_count:in_count + 5]
    terms = refs[in_count + 5:in_count + 5 + out_count]
    kc, vc, normed, attended = refs[in_count + 5 + out_count:]
    total_rows = normed.shape[0]
    heads = kc.shape[1] // HD

    @pl.when(info[1] > 0)
    def _():
        gain_row = gain[...].astype(jnp.float32)
        for first, end, block in row_spans(blocks):
            wide = block[...].astype(jnp.float32)
            mean_square = jnp.mean(wide * wide, axis=-1, keepdims=True)
            normed[first:end, :] = (
                wide * lax.rsqrt(mean_square + 1e-06) * gain_row
            ).astype(jnp.bfloat16)
        projected = jnp.dot(
            normed[...], w[...], preferred_element_type=jnp.float32
        ).astype(jnp.bfloat16)
        width = heads * HD
        start = pl.multiple_of(info[0], total_rows)
        kc[pl.ds(start, total_rows), :] = projected[:, width:2 * width]
        vc[pl.ds(start, total_rows), :] = projected[:, 2 * width:]
        for h in range(heads):
            cols = pl.ds(h * HD, HD)
            scores = lax.dot_general(
                projected[:, h * HD:(h + 1) * HD],
                kc[:, cols],
                (((1,), (1,)), ((), ())),
                preferred_element_type=jnp.float32,
            )
            top = jnp.max(scores, axis=-1, keepdims=True)
            weights = jnp.exp2((scores - top) * SCALE)
            share = 1.0 / jnp.sum(weights, axis=-1, keepdims=True)
            mixed = jnp.dot(
                weights.astype(jnp.bfloat16), vc[:, cols], preferred_element_type=jnp.float32
            )
            attended[:, cols] = (mixed * share).astype(jnp.bfloat16)
        step = wo.shape[1] // OUT_STEPS
        for i in range(OUT_STEPS):
            cols = pl.ds(i * step, step)
            product = jnp.dot(
                attended[...], wo[:, cols], preferred_element_type=jnp.float32
            ).astype(jnp.bfloat16)
            for first, end, term in row_spans(terms):
                term[:, cols] = product[first:end]

    @pl.when(info[1] <= 0)
    def _():
        for term in terms:
            term[...] = jnp.zeros_like(term)


def load_kernel(w_hbm, wo_hbm, kc_hbm, vc_hbm, gain_hbm, w, wo, kc, vc, gain, sems):
    parts, _, width = w_hbm.shape
    pairs = [(w_hbm.at[i], w.at[:, pl.ds(i * width, width)]) for i in range(parts)]
    pairs += [(wo_hbm, wo), (kc_hbm, kc), (vc_hbm, vc), (gain_hbm, gain)]
    copies = [pltpu.make_async_copy(a, b, sems.at[i]) for i, (a, b) in enumerate(pairs)]
    for copy in copies:
        copy.start()
    for copy in copies:
        copy.wait()


def loaded(w, wo, kc, vc, gain):
    parts, depth, width = w.shape
    arrays = (w, wo, kc, vc, gain)
    shapes = [(depth, parts * width)] + [a.shape for a in arrays[1:]]
    return pl.pallas_call(
        load_kernel,
        out_shape=[pltpu.VMEM(shape, w.dtype) for shape in shapes],
        in_specs=[pl.BlockSpec(memory_space=pl.ANY)] * len(arrays),
        out_specs=[pl.BlockSpec(memory_space=pltpu.VMEM)] * len(arrays),
        scratch_shapes=[pltpu.SemaphoreType.DMA((parts + 4,))],
        compiler_params=pltpu.CompilerParams(vmem_limit_bytes=VMEM_LIMIT),
        cost_estimate=pl.CostEstimate(
            flops=0, bytes_accessed=2 * sum(a.size for a in arrays), transcendentals=0
        ),
    )(*[pltpu.with_memory_space_constraint(a, pltpu.HBM) for a in arrays])


def block_terms(info, blocks, rows_out, gain, w, wo, kc, vc):
    count, width = len(blocks), blocks[0].shape[1]
    row_count = sum(rows_out)
    vmem = pl.BlockSpec(memory_space=pltpu.VMEM)
    flops = 2 * row_count * (w.size + wo.size + 2 * kc.size)
    held = [pltpu.with_memory_space_constraint(x, pltpu.VMEM) for x in (gain, w, wo, kc, vc)]
    cache = pltpu.VMEM(kc.shape, kc.dtype)
    out = pl.pallas_call(
        functools.partial(block_kernel, count, len(rows_out)),
        out_shape=[jax.ShapeDtypeStruct((rows, width), jnp.bfloat16) for rows in rows_out]
        + [cache] * 2,
        in_specs=[pl.BlockSpec(memory_space=pltpu.SMEM)] + [vmem] * (count + 5),
        out_specs=[vmem] * (len(rows_out) + 2),
        input_output_aliases={count + 4: len(rows_out), count + 5: len(rows_out) + 1},
        scratch_shapes=[
            pltpu.VMEM((row_count, width), jnp.bfloat16),
            pltpu.VMEM((row_count, kc.shape[1]), jnp.bfloat16),
        ],
        compiler_params=pltpu.CompilerParams(vmem_limit_bytes=VMEM_LIMIT),
        cost_estimate=pl.CostEstimate(
            flops=flops, bytes_accessed=2 * (w.size + wo.size), transcendentals=0
        ),
    )(info, *blocks, *held)
    return out[:-2], out[-2], out[-1]


STAY = ((0, 0), (1, 1), (2, 2), (3, 3))
NEAR = ((0, 1), (1, 0), (2, 3), (3, 2))
FAR = ((0, 3), (1, 2), (2, 1), (3, 0))


def send(block, pairs, hop=0):
    sections = lax.axis_size("section")
    n = lax.axis_size("uly")
    route = [
        (s * n + a, (s + hop) % sections * n + b) for s in range(sections) for a, b in pairs
    ]
    return lax.ppermute(block, ("section", "uly"), route)


def summed(*blocks):
    total = blocks[0].astype(jnp.float32)
    for block in blocks[1:]:
        total = total + block.astype(jnp.float32)
    return total


def summed(*blocks):
    total = blocks[0].astype(jnp.float32)
    for block in blocks[1:]:
        total = total + block.astype(jnp.float32)
    return total


def rounded(*blocks):
    return summed(*blocks).astype(jnp.bfloat16)


def behind(block, other):
    return lax.optimization_barrier((block, other))[0]


def pieces_of(rows):
    return [rows * share // sum(SHARES) for share in SHARES]


def cut(blocks, sizes):
    whole = jnp.concatenate(blocks)
    starts = [sum(sizes[:i]) for i in range(len(sizes))]
    return [whole[start:start + size] for start, size in zip(starts, sizes)]


def gathered(own, low):
    far = send(own, FAR)
    near = send(own, NEAR)
    last = send(far, NEAR)
    kept = [jnp.where(low, own, far), jnp.where(low, far, own)]
    return kept, [jnp.where(low, near, last), jnp.where(low, last, near)]


def passed_on(kept, terms, hop):
    count = len(kept)
    pairs, fars, updated = [], [], []

    def finish(i, *others):
        far = behind(fars[i], *others) if others else fars[i]
        updated.append(rounded(kept[i], pairs[i], far))

    for i in range(count):
        partners = terms[count + i]
        if i > 0:
            partners = behind(partners, updated[i - 2] if i > 1 else pairs[0])
        pairs.append(rounded(terms[i], send(partners, NEAR)))
        fars.append(send(pairs[i], FAR))
        if i > 0:
            finish(i - 1, pairs[i])
    finish(count - 1)
    others = [send(block, NEAR, hop) for block in updated]
    return [send(block, STAY, hop) if hop else block for block in updated], others


def delivered(kept, terms, low):
    first, second, near_first, near_second = terms
    last = send(jnp.where(low, near_second, near_first), NEAR)
    before = jnp.where(low, *cut(kept, [first.shape[0], second.shape[0]]))
    base = send(rounded(before, jnp.where(low, first, second)), STAY, 1)
    pair = rounded(jnp.where(low, second, first), last)
    near, pair = lax.optimization_barrier((jnp.where(low, near_first, near_second), pair))
    far = send(pair, FAR, 1)
    near = send(near, NEAR, 1)
    return rounded(base, far, near)


def shards(
    state, patch_slot, section_active, qkv_weight, out_weight, norm_gain, stale_keys, stale_values
):
    section_count = lax.axis_size("section")
    section_index = lax.axis_index("section")
    block_count = section_active[0]
    n = lax.axis_size("uly")
    low = lax.axis_index("uly") < n // 2
    shard_rows = state.shape[1]
    patch_rows = shard_rows * n
    stored = (
        jnp.transpose(qkv_weight[0], (1, 0, 2)),
        out_weight[0],
        stale_keys[0],
        stale_values[0],
        norm_gain,
    )
    w, wo, kc, vc, gain = loaded(*stored)
    kept, others = gathered(state[0], low)
    sizes = pieces_of(patch_rows // 2)
    for tick in range(TICKS):
        slot = patch_slot[(section_index - tick) % section_count]
        for index in range(PASSES):
            applies = block_count > index
            info = jnp.stack([slot * patch_rows, applies.astype(jnp.int32)])
            last = index == PASSES - 1
            final = last and tick == TICKS - 1
            rows_out = [shard_rows] * n if final else sizes * 2
            terms, kc, vc = block_terms(info, kept + others, rows_out, gain, w, wo, kc, vc)
            if final:
                return delivered(kept, terms, low)[None]
            kept = cut(kept, sizes) if tick + index == 0 else kept
            kept, others = passed_on(kept, terms, 1 if last else 0)


def solution(mesh):
    return jax.shard_map(
        shards,
        mesh=mesh,
        in_specs=(
            P("section", "uly", None),
            P(),
            P("section"),
            P("section", None, None, "uly"),
            P("section", "uly", None),
            P("section", None),
            P("section", None, "uly"),
            P("section", None, "uly"),
        ),
        out_specs=P("section", "uly", None),
        check_vma=False,
    )
```

```python
import functools
import math

import jax
import jax.numpy as jnp
from jax import lax
from jax.experimental import pallas as pl
from jax.experimental.pallas import tpu as pltpu
from jax.sharding import PartitionSpec as P

HD = 128
TICKS = 3
PASSES = 2
VMEM_LIMIT = 12 * 2**20
SCALE = HD ** (-0.5) * math.log2(math.e)
OUT_STEPS = 3
SHARES = (1, 1)


def row_spans(refs):
    start = 0
    for ref in refs:
        yield start, start + ref.shape[0], ref
        start += ref.shape[0]


def block_kernel(in_count, out_count, info, *refs):
    blocks = refs[:in_count]
    gain, w, wo, _, _ = refs[in_count:in_count + 5]
    terms = refs[in_count + 5:in_count + 5 + out_count]
    kc, vc, normed, attended = refs[in_count + 5 + out_count:]
    total_rows = normed.shape[0]
    heads = kc.shape[1] // HD

    @pl.when(info[1] > 0)
    def _():
        gain_row = gain[...].astype(jnp.float32)
        for first, end, block in row_spans(blocks):
            wide = block[...].astype(jnp.float32)
            mean_square = jnp.mean(wide * wide, axis=-1, keepdims=True)
            normed[first:end, :] = (
                wide * lax.rsqrt(mean_square + 1e-06) * gain_row
            ).astype(jnp.bfloat16)
        projected = jnp.dot(
            normed[...], w[...], preferred_element_type=jnp.float32
        ).astype(jnp.bfloat16)
        width = heads * HD
        start = pl.multiple_of(info[0], total_rows)
        kc[pl.ds(start, total_rows), :] = projected[:, width:2 * width]
        vc[pl.ds(start, total_rows), :] = projected[:, 2 * width:]
        for h in range(heads):
            cols = pl.ds(h * HD, HD)
            scores = lax.dot_general(
                projected[:, h * HD:(h + 1) * HD],
                kc[:, cols],
                (((1,), (1,)), ((), ())),
                preferred_element_type=jnp.float32,
            )
            top = jnp.max(scores, axis=-1, keepdims=True)
            weights = jnp.exp2((scores - top) * SCALE)
            share = 1.0 / jnp.sum(weights, axis=-1, keepdims=True)
            mixed = jnp.dot(
                weights.astype(jnp.bfloat16), vc[:, cols], preferred_element_type=jnp.float32
            )
            attended[:, cols] = (mixed * share).astype(jnp.bfloat16)
        step = wo.shape[1] // OUT_STEPS
        for i in range(OUT_STEPS):
            cols = pl.ds(i * step, step)
            product = jnp.dot(
                attended[...], wo[:, cols], preferred_element_type=jnp.float32
            ).astype(jnp.bfloat16)
            for first, end, term in row_spans(terms):
                term[:, cols] = product[first:end]

    @pl.when(info[1] <= 0)
    def _():
        for term in terms:
            term[...] = jnp.zeros_like(term)


def load_kernel(w_hbm, wo_hbm, kc_hbm, vc_hbm, gain_hbm, w, wo, kc, vc, gain, sems):
    parts, _, width = w_hbm.shape
    pairs = [(w_hbm.at[i], w.at[:, pl.ds(i * width, width)]) for i in range(parts)]
    pairs += [(wo_hbm, wo), (kc_hbm, kc), (vc_hbm, vc), (gain_hbm, gain)]
    copies = [pltpu.make_async_copy(a, b, sems.at[i]) for i, (a, b) in enumerate(pairs)]
    for copy in copies:
        copy.start()
    for copy in copies:
        copy.wait()


def loaded(w, wo, kc, vc, gain):
    parts, depth, width = w.shape
    arrays = (w, wo, kc, vc, gain)
    shapes = [(depth, parts * width)] + [a.shape for a in arrays[1:]]
    return pl.pallas_call(
        load_kernel,
        out_shape=[pltpu.VMEM(shape, w.dtype) for shape in shapes],
        in_specs=[pl.BlockSpec(memory_space=pl.ANY)] * len(arrays),
        out_specs=[pl.BlockSpec(memory_space=pltpu.VMEM)] * len(arrays),
        scratch_shapes=[pltpu.SemaphoreType.DMA((parts + 4,))],
        compiler_params=pltpu.CompilerParams(vmem_limit_bytes=VMEM_LIMIT),
        cost_estimate=pl.CostEstimate(
            flops=0, bytes_accessed=2 * sum(a.size for a in arrays), transcendentals=0
        ),
    )(*[pltpu.with_memory_space_constraint(a, pltpu.HBM) for a in arrays])


def block_terms(info, blocks, rows_out, gain, w, wo, kc, vc):
    count, width = len(blocks), blocks[0].shape[1]
    row_count = sum(rows_out)
    vmem = pl.BlockSpec(memory_space=pltpu.VMEM)
    flops = 2 * row_count * (w.size + wo.size + 2 * kc.size)
    held = [pltpu.with_memory_space_constraint(x, pltpu.VMEM) for x in (gain, w, wo, kc, vc)]
    cache = pltpu.VMEM(kc.shape, kc.dtype)
    out = pl.pallas_call(
        functools.partial(block_kernel, count, len(rows_out)),
        out_shape=[jax.ShapeDtypeStruct((rows, width), jnp.bfloat16) for rows in rows_out]
        + [cache] * 2,
        in_specs=[pl.BlockSpec(memory_space=pltpu.SMEM)] + [vmem] * (count + 5),
        out_specs=[vmem] * (len(rows_out) + 2),
        input_output_aliases={count + 4: len(rows_out), count + 5: len(rows_out) + 1},
        scratch_shapes=[
            pltpu.VMEM((row_count, width), jnp.bfloat16),
            pltpu.VMEM((row_count, kc.shape[1]), jnp.bfloat16),
        ],
        compiler_params=pltpu.CompilerParams(vmem_limit_bytes=VMEM_LIMIT),
        cost_estimate=pl.CostEstimate(
            flops=flops, bytes_accessed=2 * (w.size + wo.size), transcendentals=0
        ),
    )(info, *blocks, *held)
    return out[:-2], out[-2], out[-1]


STAY = ((0, 0), (1, 1), (2, 2), (3, 3))
NEAR = ((0, 1), (1, 0), (2, 3), (3, 2))
FAR = ((0, 3), (1, 2), (2, 1), (3, 0))
CROSS = ((0, 2), (1, 3), (2, 0), (3, 1))


def send(block, pairs, hop=0):
    sections = lax.axis_size("section")
    n = lax.axis_size("uly")
    route = [
        (s * n + a, (s + hop) % sections * n + b) for s in range(sections) for a, b in pairs
    ]
    return lax.ppermute(block, ("section", "uly"), route)


def summed(*blocks):
    total = blocks[0].astype(jnp.float32)
    for block in blocks[1:]:
        total = total + block.astype(jnp.float32)
    return total


def summed(*blocks):
    total = blocks[0].astype(jnp.float32)
    for block in blocks[1:]:
        total = total + block.astype(jnp.float32)
    return total


def rounded(*blocks):
    return summed(*blocks).astype(jnp.bfloat16)


def behind(block, other):
    return lax.optimization_barrier((block, other))[0]


def pieces_of(rows):
    return [rows * share // sum(SHARES) for share in SHARES]


def cut(blocks, sizes):
    whole = jnp.concatenate(blocks)
    starts = [sum(sizes[:i]) for i in range(len(sizes))]
    return [whole[start:start + size] for start, size in zip(starts, sizes)]


def gathered(own, low):
    far = send(own, FAR)
    near = send(own, NEAR)
    last = send(far, NEAR)
    kept = [jnp.where(low, own, far), jnp.where(low, far, own)]
    return kept, [jnp.where(low, near, last), jnp.where(low, last, near)]


def passed_on(kept, terms, hop):
    count = len(kept)
    next_kept, next_others = [], []
    pair = None
    for current, mine, partners in zip(kept, terms[:count], terms[count:]):
        partners = partners if pair is None else behind(partners, pair)
        pair = rounded(mine, send(partners, NEAR))
        updated = rounded(current, pair, send(pair, FAR))
        next_others.append(send(updated, NEAR, hop))
        next_kept.append(send(updated, STAY, hop) if hop else updated)
    return next_kept, next_others


def delivered(kept, terms, low):
    first, second, near_first, near_second = terms
    before = jnp.where(low, *cut(kept, [first.shape[0], second.shape[0]]))
    cross = send(jnp.where(low, near_second, near_first), CROSS, 1)
    far = send(jnp.where(low, second, first), FAR, 1)
    near = send(jnp.where(low, near_first, near_second), NEAR, 1)
    base = send(rounded(before, jnp.where(low, first, second)), STAY, 1)
    return rounded(base, near, far, cross)


def shards(
    state, patch_slot, section_active, qkv_weight, out_weight, norm_gain, stale_keys, stale_values
):
    section_count = lax.axis_size("section")
    section_index = lax.axis_index("section")
    block_count = section_active[0]
    n = lax.axis_size("uly")
    low = lax.axis_index("uly") < n // 2
    shard_rows = state.shape[1]
    patch_rows = shard_rows * n
    stored = (
        jnp.transpose(qkv_weight[0], (1, 0, 2)),
        out_weight[0],
        stale_keys[0],
        stale_values[0],
        norm_gain,
    )
    w, wo, kc, vc, gain = loaded(*stored)
    kept, others = gathered(state[0], low)
    sizes = pieces_of(patch_rows // 2)
    for tick in range(TICKS):
        slot = patch_slot[(section_index - tick) % section_count]
        for index in range(PASSES):
            applies = block_count > index
            info = jnp.stack([slot * patch_rows, applies.astype(jnp.int32)])
            last = index == PASSES - 1
            final = last and tick == TICKS - 1
            rows_out = [shard_rows] * n if final else sizes * 2
            terms, kc, vc = block_terms(info, kept + others, rows_out, gain, w, wo, kc, vc)
            if final:
                return delivered(kept, terms, low)[None]
            kept = cut(kept, sizes) if tick + index == 0 else kept
            kept, others = passed_on(kept, terms, 1 if last else 0)


def solution(mesh):
    return jax.shard_map(
        shards,
        mesh=mesh,
        in_specs=(
            P("section", "uly", None),
            P(),
            P("section"),
            P("section", None, None, "uly"),
            P("section", "uly", None),
            P("section", None),
            P("section", None, "uly"),
            P("section", None, "uly"),
        ),
        out_specs=P("section", "uly", None),
        check_vma=False,
    )
```

```python
import functools
import math

import jax
import jax.numpy as jnp
from jax import lax
from jax.experimental import pallas as pl
from jax.experimental.pallas import tpu as pltpu
from jax.sharding import PartitionSpec as P

HD = 128
TICKS = 3
PASSES = 2
VMEM_LIMIT = 12 * 2**20
SCALE = HD ** (-0.5) * math.log2(math.e)
OUT_STEPS = 3
SHARES = (1, 1)


def row_spans(refs):
    start = 0
    for ref in refs:
        yield start, start + ref.shape[0], ref
        start += ref.shape[0]


def block_kernel(in_count, out_count, info, *refs):
    blocks = refs[:in_count]
    gain, w, wo, _, _ = refs[in_count:in_count + 5]
    terms = refs[in_count + 5:in_count + 5 + out_count]
    kc, vc, gained, attended = refs[in_count + 5 + out_count:]
    total_rows = gained.shape[0]
    heads = kc.shape[1] // HD

    @pl.when(info[1] > 0)
    def _():
        gain_row = gain[...].astype(jnp.float32)
        factors = []
        for first, end, block in row_spans(blocks):
            wide = block[...].astype(jnp.float32)
            mean_square = jnp.mean(wide * wide, axis=-1, keepdims=True)
            factors.append(lax.rsqrt(mean_square + 1e-06))
            gained[first:end, :] = (wide * gain_row).astype(jnp.bfloat16)
        projected = jnp.dot(gained[...], w[...], preferred_element_type=jnp.float32)
        projected = (projected * jnp.concatenate(factors)).astype(jnp.bfloat16)
        width = heads * HD
        start = pl.multiple_of(info[0], total_rows)
        kc[pl.ds(start, total_rows), :] = projected[:, width:2 * width]
        vc[pl.ds(start, total_rows), :] = projected[:, 2 * width:]
        for h in range(heads):
            cols = pl.ds(h * HD, HD)
            scores = lax.dot_general(
                projected[:, h * HD:(h + 1) * HD],
                kc[:, cols],
                (((1,), (1,)), ((), ())),
                preferred_element_type=jnp.float32,
            )
            top = jnp.max(scores, axis=-1, keepdims=True)
            weights = jnp.exp2((scores - top) * SCALE)
            share = 1.0 / jnp.sum(weights, axis=-1, keepdims=True)
            mixed = jnp.dot(
                weights.astype(jnp.bfloat16), vc[:, cols], preferred_element_type=jnp.float32
            )
            attended[:, cols] = (mixed * share).astype(jnp.bfloat16)
        step = wo.shape[1] // OUT_STEPS
        for i in range(OUT_STEPS):
            cols = pl.ds(i * step, step)
            product = jnp.dot(
                attended[...], wo[:, cols], preferred_element_type=jnp.float32
            ).astype(jnp.bfloat16)
            for first, end, term in row_spans(terms):
                term[:, cols] = product[first:end]

    @pl.when(info[1] <= 0)
    def _():
        for term in terms:
            term[...] = jnp.zeros_like(term)


def load_kernel(w_hbm, wo_hbm, kc_hbm, vc_hbm, gain_hbm, w, wo, kc, vc, gain, sems):
    parts, _, width = w_hbm.shape
    pairs = [(w_hbm.at[i], w.at[:, pl.ds(i * width, width)]) for i in range(parts)]
    pairs += [(wo_hbm, wo), (kc_hbm, kc), (vc_hbm, vc), (gain_hbm, gain)]
    copies = [pltpu.make_async_copy(a, b, sems.at[i]) for i, (a, b) in enumerate(pairs)]
    for copy in copies:
        copy.start()
    for copy in copies:
        copy.wait()


def loaded(w, wo, kc, vc, gain):
    parts, depth, width = w.shape
    arrays = (w, wo, kc, vc, gain)
    shapes = [(depth, parts * width)] + [a.shape for a in arrays[1:]]
    return pl.pallas_call(
        load_kernel,
        out_shape=[pltpu.VMEM(shape, w.dtype) for shape in shapes],
        in_specs=[pl.BlockSpec(memory_space=pl.ANY)] * len(arrays),
        out_specs=[pl.BlockSpec(memory_space=pltpu.VMEM)] * len(arrays),
        scratch_shapes=[pltpu.SemaphoreType.DMA((parts + 4,))],
        compiler_params=pltpu.CompilerParams(vmem_limit_bytes=VMEM_LIMIT),
        cost_estimate=pl.CostEstimate(
            flops=0, bytes_accessed=2 * sum(a.size for a in arrays), transcendentals=0
        ),
    )(*[pltpu.with_memory_space_constraint(a, pltpu.HBM) for a in arrays])


def block_terms(info, blocks, rows_out, gain, w, wo, kc, vc):
    count, width = len(blocks), blocks[0].shape[1]
    row_count = sum(rows_out)
    vmem = pl.BlockSpec(memory_space=pltpu.VMEM)
    flops = 2 * row_count * (w.size + wo.size + 2 * kc.size)
    held = [pltpu.with_memory_space_constraint(x, pltpu.VMEM) for x in (gain, w, wo, kc, vc)]
    cache = pltpu.VMEM(kc.shape, kc.dtype)
    out = pl.pallas_call(
        functools.partial(block_kernel, count, len(rows_out)),
        out_shape=[jax.ShapeDtypeStruct((rows, width), jnp.bfloat16) for rows in rows_out]
        + [cache] * 2,
        in_specs=[pl.BlockSpec(memory_space=pltpu.SMEM)] + [vmem] * (count + 5),
        out_specs=[vmem] * (len(rows_out) + 2),
        input_output_aliases={count + 4: len(rows_out), count + 5: len(rows_out) + 1},
        scratch_shapes=[
            pltpu.VMEM((row_count, width), jnp.bfloat16),
            pltpu.VMEM((row_count, kc.shape[1]), jnp.bfloat16),
        ],
        compiler_params=pltpu.CompilerParams(vmem_limit_bytes=VMEM_LIMIT),
        cost_estimate=pl.CostEstimate(
            flops=flops, bytes_accessed=2 * (w.size + wo.size), transcendentals=0
        ),
    )(info, *blocks, *held)
    return out[:-2], out[-2], out[-1]


STAY = ((0, 0), (1, 1), (2, 2), (3, 3))
NEAR = ((0, 1), (1, 0), (2, 3), (3, 2))
FAR = ((0, 3), (1, 2), (2, 1), (3, 0))
CROSS = ((0, 2), (1, 3), (2, 0), (3, 1))


def send(block, pairs, hop=0):
    sections = lax.axis_size("section")
    n = lax.axis_size("uly")
    route = [
        (s * n + a, (s + hop) % sections * n + b) for s in range(sections) for a, b in pairs
    ]
    return lax.ppermute(block, ("section", "uly"), route)


def summed(*blocks):
    total = blocks[0].astype(jnp.float32)
    for block in blocks[1:]:
        total = total + block.astype(jnp.float32)
    return total


def summed(*blocks):
    total = blocks[0].astype(jnp.float32)
    for block in blocks[1:]:
        total = total + block.astype(jnp.float32)
    return total


def rounded(*blocks):
    return summed(*blocks).astype(jnp.bfloat16)


def behind(block, other):
    return lax.optimization_barrier((block, other))[0]


def pieces_of(rows):
    return [rows * share // sum(SHARES) for share in SHARES]


def cut(blocks, sizes):
    whole = jnp.concatenate(blocks)
    starts = [sum(sizes[:i]) for i in range(len(sizes))]
    return [whole[start:start + size] for start, size in zip(starts, sizes)]


def gathered(own, low):
    far = send(own, FAR)
    near = send(own, NEAR)
    last = send(far, NEAR)
    kept = [jnp.where(low, own, far), jnp.where(low, far, own)]
    return kept, [jnp.where(low, near, last), jnp.where(low, last, near)]


def passed_on(kept, terms, hop):
    count = len(kept)
    next_kept, next_others = [], []
    pair = None
    for current, mine, partners in zip(kept, terms[:count], terms[count:]):
        partners = partners if pair is None else behind(partners, pair)
        pair = rounded(mine, send(partners, NEAR))
        updated = rounded(current, pair, send(pair, FAR))
        next_others.append(send(updated, NEAR, hop))
        next_kept.append(send(updated, STAY, hop) if hop else updated)
    return next_kept, next_others


def delivered(kept, terms, low):
    first, second, near_first, near_second = terms
    before = jnp.where(low, *cut(kept, [first.shape[0], second.shape[0]]))
    cross = send(jnp.where(low, near_second, near_first), CROSS, 1)
    far = send(jnp.where(low, second, first), FAR, 1)
    near = send(jnp.where(low, near_first, near_second), NEAR, 1)
    base = send(rounded(before, jnp.where(low, first, second)), STAY, 1)
    return rounded(base, near, far, cross)


def shards(
    state, patch_slot, section_active, qkv_weight, out_weight, norm_gain, stale_keys, stale_values
):
    section_count = lax.axis_size("section")
    section_index = lax.axis_index("section")
    block_count = section_active[0]
    n = lax.axis_size("uly")
    low = lax.axis_index("uly") < n // 2
    shard_rows = state.shape[1]
    patch_rows = shard_rows * n
    stored = (
        jnp.transpose(qkv_weight[0], (1, 0, 2)),
        out_weight[0],
        stale_keys[0],
        stale_values[0],
        norm_gain,
    )
    w, wo, kc, vc, gain = loaded(*stored)
    kept, others = gathered(state[0], low)
    sizes = pieces_of(patch_rows // 2)
    for tick in range(TICKS):
        slot = patch_slot[(section_index - tick) % section_count]
        for index in range(PASSES):
            applies = block_count > index
            info = jnp.stack([slot * patch_rows, applies.astype(jnp.int32)])
            last = index == PASSES - 1
            final = last and tick == TICKS - 1
            rows_out = [shard_rows] * n if final else sizes * 2
            terms, kc, vc = block_terms(info, kept + others, rows_out, gain, w, wo, kc, vc)
            if final:
                return delivered(kept, terms, low)[None]
            kept = cut(kept, sizes) if tick + index == 0 else kept
            kept, others = passed_on(kept, terms, 1 if last else 0)


def solution(mesh):
    return jax.shard_map(
        shards,
        mesh=mesh,
        in_specs=(
            P("section", "uly", None),
            P(),
            P("section"),
            P("section", None, None, "uly"),
            P("section", "uly", None),
            P("section", None),
            P("section", None, "uly"),
            P("section", None, "uly"),
        ),
        out_specs=P("section", "uly", None),
        check_vma=False,
    )
```

```python
import functools
import math

import jax
import jax.numpy as jnp
from jax import lax
from jax.experimental import pallas as pl
from jax.experimental.pallas import tpu as pltpu
from jax.sharding import PartitionSpec as P

HD = 128
TICKS = 3
PASSES = 2
VMEM_LIMIT = 12 * 2**20
SCALE = HD ** (-0.5) * math.log2(math.e)
OUT_STEPS = 3
SHARES = (1, 1)


def row_spans(refs):
    start = 0
    for ref in refs:
        yield start, start + ref.shape[0], ref
        start += ref.shape[0]


def block_kernel(in_count, out_count, info, *refs):
    blocks = refs[:in_count]
    gain, w, wo, _, _ = refs[in_count:in_count + 5]
    terms = refs[in_count + 5:in_count + 5 + out_count]
    kc, vc, gained, attended = refs[in_count + 5 + out_count:]
    total_rows = gained.shape[0]
    heads = kc.shape[1] // HD

    @pl.when(info[1] > 0)
    def _():
        gain_row = gain[...].astype(jnp.float32)
        factors = []
        for first, end, block in row_spans(blocks):
            wide = block[...].astype(jnp.float32)
            mean_square = jnp.mean(wide * wide, axis=-1, keepdims=True)
            factors.append(lax.rsqrt(mean_square + 1e-06))
            gained[first:end, :] = (wide * gain_row).astype(jnp.bfloat16)
        projected = jnp.dot(gained[...], w[...], preferred_element_type=jnp.float32)
        projected = (projected * jnp.concatenate(factors)).astype(jnp.bfloat16)
        width = heads * HD
        start = pl.multiple_of(info[0], total_rows)
        kc[pl.ds(start, total_rows), :] = projected[:, width:2 * width]
        vc[pl.ds(start, total_rows), :] = projected[:, 2 * width:]
        for h in range(heads):
            cols = pl.ds(h * HD, HD)
            scores = lax.dot_general(
                projected[:, h * HD:(h + 1) * HD],
                kc[:, cols],
                (((1,), (1,)), ((), ())),
                preferred_element_type=jnp.float32,
            )
            top = jnp.max(scores, axis=-1, keepdims=True)
            weights = jnp.exp2((scores - top) * SCALE)
            share = 1.0 / jnp.sum(weights, axis=-1, keepdims=True)
            mixed = jnp.dot(
                weights.astype(jnp.bfloat16), vc[:, cols], preferred_element_type=jnp.float32
            )
            attended[:, cols] = (mixed * share).astype(jnp.bfloat16)
        step = wo.shape[1] // OUT_STEPS
        for i in range(OUT_STEPS):
            cols = pl.ds(i * step, step)
            product = jnp.dot(
                attended[...], wo[:, cols], preferred_element_type=jnp.float32
            ).astype(jnp.bfloat16)
            for first, end, term in row_spans(terms):
                term[:, cols] = product[first:end]

    @pl.when(info[1] <= 0)
    def _():
        for term in terms:
            term[...] = jnp.zeros_like(term)


def load_kernel(w_hbm, wo_hbm, kc_hbm, vc_hbm, gain_hbm, w, wo, kc, vc, gain, sems):
    parts, _, width = w_hbm.shape
    pairs = [(w_hbm.at[i], w.at[:, pl.ds(i * width, width)]) for i in range(parts)]
    pairs += [(wo_hbm, wo), (kc_hbm, kc), (vc_hbm, vc), (gain_hbm, gain)]
    copies = [pltpu.make_async_copy(a, b, sems.at[i]) for i, (a, b) in enumerate(pairs)]
    for copy in copies:
        copy.start()
    for copy in copies:
        copy.wait()


def loaded(w, wo, kc, vc, gain):
    parts, depth, width = w.shape
    arrays = (w, wo, kc, vc, gain)
    shapes = [(depth, parts * width)] + [a.shape for a in arrays[1:]]
    return pl.pallas_call(
        load_kernel,
        out_shape=[pltpu.VMEM(shape, w.dtype) for shape in shapes],
        in_specs=[pl.BlockSpec(memory_space=pl.ANY)] * len(arrays),
        out_specs=[pl.BlockSpec(memory_space=pltpu.VMEM)] * len(arrays),
        scratch_shapes=[pltpu.SemaphoreType.DMA((parts + 4,))],
        compiler_params=pltpu.CompilerParams(vmem_limit_bytes=VMEM_LIMIT),
        cost_estimate=pl.CostEstimate(
            flops=0, bytes_accessed=2 * sum(a.size for a in arrays), transcendentals=0
        ),
    )(*[pltpu.with_memory_space_constraint(a, pltpu.HBM) for a in arrays])


def block_terms(info, blocks, rows_out, gain, w, wo, kc, vc):
    count, width = len(blocks), blocks[0].shape[1]
    row_count = sum(rows_out)
    vmem = pl.BlockSpec(memory_space=pltpu.VMEM)
    flops = 2 * row_count * (w.size + wo.size + 2 * kc.size)
    held = [pltpu.with_memory_space_constraint(x, pltpu.VMEM) for x in (gain, w, wo, kc, vc)]
    cache = pltpu.VMEM(kc.shape, kc.dtype)
    out = pl.pallas_call(
        functools.partial(block_kernel, count, len(rows_out)),
        out_shape=[jax.ShapeDtypeStruct((rows, width), jnp.bfloat16) for rows in rows_out]
        + [cache] * 2,
        in_specs=[pl.BlockSpec(memory_space=pltpu.SMEM)] + [vmem] * (count + 5),
        out_specs=[vmem] * (len(rows_out) + 2),
        input_output_aliases={count + 4: len(rows_out), count + 5: len(rows_out) + 1},
        scratch_shapes=[
            pltpu.VMEM((row_count, width), jnp.bfloat16),
            pltpu.VMEM((row_count, kc.shape[1]), jnp.bfloat16),
        ],
        compiler_params=pltpu.CompilerParams(vmem_limit_bytes=VMEM_LIMIT),
        cost_estimate=pl.CostEstimate(
            flops=flops, bytes_accessed=2 * (w.size + wo.size), transcendentals=0
        ),
    )(info, *blocks, *held)
    return out[:-2], out[-2], out[-1]


STAY = ((0, 0), (1, 1), (2, 2), (3, 3))
NEAR = ((0, 1), (1, 0), (2, 3), (3, 2))
FAR = ((0, 3), (1, 2), (2, 1), (3, 0))
CROSS = ((0, 2), (1, 3), (2, 0), (3, 1))


def send(block, pairs, hop=0):
    sections = lax.axis_size("section")
    n = lax.axis_size("uly")
    route = [
        (s * n + a, (s + hop) % sections * n + b) for s in range(sections) for a, b in pairs
    ]
    return lax.ppermute(block, ("section", "uly"), route)


def summed(*blocks):
    total = blocks[0].astype(jnp.float32)
    for block in blocks[1:]:
        total = total + block.astype(jnp.float32)
    return total


def summed(*blocks):
    total = blocks[0].astype(jnp.float32)
    for block in blocks[1:]:
        total = total + block.astype(jnp.float32)
    return total


def rounded(*blocks):
    return summed(*blocks).astype(jnp.bfloat16)


def behind(block, other):
    return lax.optimization_barrier((block, other))[0]


def pieces_of(rows):
    return [rows * share // sum(SHARES) for share in SHARES]


def cut(blocks, sizes):
    whole = jnp.concatenate(blocks)
    starts = [sum(sizes[:i]) for i in range(len(sizes))]
    return [whole[start:start + size] for start, size in zip(starts, sizes)]


def gathered(own, low):
    far = send(own, FAR)
    near = send(own, NEAR)
    last = send(far, NEAR)
    kept = [jnp.where(low, own, far), jnp.where(low, far, own)]
    return kept, [jnp.where(low, near, last), jnp.where(low, last, near)]


def passed_on(kept, terms, hop):
    count = len(kept)
    next_kept, next_others = [], []
    pair = None
    for current, mine, partners in zip(kept, terms[:count], terms[count:]):
        partners = partners if pair is None else behind(partners, pair)
        pair = rounded(mine, send(partners, NEAR))
        updated = rounded(current, pair, send(pair, FAR))
        next_others.append(send(updated, NEAR, hop))
        next_kept.append(send(updated, STAY, hop) if hop else updated)
    return next_kept, next_others


def delivered(kept, terms, low):
    first, second, near_first, near_second = terms
    before = jnp.where(low, *cut(kept, [first.shape[0], second.shape[0]]))
    cross = send(jnp.where(low, near_second, near_first), CROSS, 1)
    far = send(jnp.where(low, second, first), FAR, 1)
    near = send(jnp.where(low, near_first, near_second), NEAR, 1)
    base = send(rounded(before, jnp.where(low, first, second)), STAY, 1)
    total = lax.optimization_barrier(summed(cross))
    for block in (far, near):
        total = lax.optimization_barrier(total + block.astype(jnp.float32))
    return (total + base.astype(jnp.float32)).astype(jnp.bfloat16)


def shards(
    state, patch_slot, section_active, qkv_weight, out_weight, norm_gain, stale_keys, stale_values
):
    section_count = lax.axis_size("section")
    section_index = lax.axis_index("section")
    block_count = section_active[0]
    n = lax.axis_size("uly")
    low = lax.axis_index("uly") < n // 2
    shard_rows = state.shape[1]
    patch_rows = shard_rows * n
    stored = (
        jnp.transpose(qkv_weight[0], (1, 0, 2)),
        out_weight[0],
        stale_keys[0],
        stale_values[0],
        norm_gain,
    )
    w, wo, kc, vc, gain = loaded(*stored)
    kept, others = gathered(state[0], low)
    sizes = pieces_of(patch_rows // 2)
    for tick in range(TICKS):
        slot = patch_slot[(section_index - tick) % section_count]
        for index in range(PASSES):
            applies = block_count > index
            info = jnp.stack([slot * patch_rows, applies.astype(jnp.int32)])
            last = index == PASSES - 1
            final = last and tick == TICKS - 1
            rows_out = [shard_rows] * n if final else sizes * 2
            terms, kc, vc = block_terms(info, kept + others, rows_out, gain, w, wo, kc, vc)
            if final:
                return delivered(kept, terms, low)[None]
            kept = cut(kept, sizes) if tick + index == 0 else kept
            kept, others = passed_on(kept, terms, 1 if last else 0)


def solution(mesh):
    return jax.shard_map(
        shards,
        mesh=mesh,
        in_specs=(
            P("section", "uly", None),
            P(),
            P("section"),
            P("section", None, None, "uly"),
            P("section", "uly", None),
            P("section", None),
            P("section", None, "uly"),
            P("section", None, "uly"),
        ),
        out_specs=P("section", "uly", None),
        check_vma=False,
    )
```

```python
import functools
import math

import jax
import jax.numpy as jnp
from jax import lax
from jax.experimental import pallas as pl
from jax.experimental.pallas import tpu as pltpu
from jax.sharding import PartitionSpec as P

HD = 128
TICKS = 3
PASSES = 2
VMEM_LIMIT = 12 * 2**20
SCALE = HD ** (-0.5) * math.log2(math.e)
OUT_STEPS = 3


def row_spans(refs):
    start = 0
    for ref in refs:
        yield start, start + ref.shape[0], ref
        start += ref.shape[0]


def block_kernel(in_count, out_count, info, *refs):
    blocks = refs[:in_count]
    gain, w, wo, _, _ = refs[in_count:in_count + 5]
    terms = refs[in_count + 5:in_count + 5 + out_count]
    kc, vc, gained, attended = refs[in_count + 5 + out_count:]
    total_rows = gained.shape[0]
    heads = kc.shape[1] // HD

    @pl.when(info[1] > 0)
    def _():
        gain_row = gain[...].astype(jnp.float32)
        factors = []
        for first, end, block in row_spans(blocks):
            wide = block[...].astype(jnp.float32)
            mean_square = jnp.mean(wide * wide, axis=-1, keepdims=True)
            factors.append(lax.rsqrt(mean_square + 1e-06))
            gained[first:end, :] = (wide * gain_row).astype(jnp.bfloat16)
        projected = jnp.dot(gained[...], w[...], preferred_element_type=jnp.float32)
        projected = (projected * jnp.concatenate(factors)).astype(jnp.bfloat16)
        width = heads * HD
        start = pl.multiple_of(info[0], total_rows)
        kc[pl.ds(start, total_rows), :] = projected[:, width:2 * width]
        vc[pl.ds(start, total_rows), :] = projected[:, 2 * width:]
        for h in range(heads):
            cols = pl.ds(h * HD, HD)
            scores = lax.dot_general(
                projected[:, h * HD:(h + 1) * HD],
                kc[:, cols],
                (((1,), (1,)), ((), ())),
                preferred_element_type=jnp.float32,
            )
            top = jnp.max(scores, axis=-1, keepdims=True)
            weights = jnp.exp2((scores - top) * SCALE)
            share = 1.0 / jnp.sum(weights, axis=-1, keepdims=True)
            mixed = jnp.dot(
                weights.astype(jnp.bfloat16), vc[:, cols], preferred_element_type=jnp.float32
            )
            attended[:, cols] = (mixed * share).astype(jnp.bfloat16)
        step = wo.shape[1] // OUT_STEPS
        for i in range(OUT_STEPS):
            cols = pl.ds(i * step, step)
            product = jnp.dot(
                attended[...], wo[:, cols], preferred_element_type=jnp.float32
            ).astype(jnp.bfloat16)
            for first, end, term in row_spans(terms):
                term[:, cols] = product[first:end]

    @pl.when(info[1] <= 0)
    def _():
        for term in terms:
            term[...] = jnp.zeros_like(term)


def load_kernel(w_hbm, wo_hbm, kc_hbm, vc_hbm, gain_hbm, w, wo, kc, vc, gain, sems):
    parts, _, width = w_hbm.shape
    pairs = [(w_hbm.at[i], w.at[:, pl.ds(i * width, width)]) for i in range(parts)]
    pairs += [(wo_hbm, wo), (kc_hbm, kc), (vc_hbm, vc), (gain_hbm, gain)]
    copies = [pltpu.make_async_copy(a, b, sems.at[i]) for i, (a, b) in enumerate(pairs)]
    for copy in copies:
        copy.start()
    for copy in copies:
        copy.wait()


def loaded(w, wo, kc, vc, gain):
    parts, depth, width = w.shape
    arrays = (w, wo, kc, vc, gain)
    shapes = [(depth, parts * width)] + [a.shape for a in arrays[1:]]
    return pl.pallas_call(
        load_kernel,
        out_shape=[pltpu.VMEM(shape, w.dtype) for shape in shapes],
        in_specs=[pl.BlockSpec(memory_space=pl.ANY)] * len(arrays),
        out_specs=[pl.BlockSpec(memory_space=pltpu.VMEM)] * len(arrays),
        scratch_shapes=[pltpu.SemaphoreType.DMA((parts + 4,))],
        compiler_params=pltpu.CompilerParams(vmem_limit_bytes=VMEM_LIMIT),
        cost_estimate=pl.CostEstimate(
            flops=0, bytes_accessed=2 * sum(a.size for a in arrays), transcendentals=0
        ),
    )(*[pltpu.with_memory_space_constraint(a, pltpu.HBM) for a in arrays])


def block_terms(info, blocks, rows_out, gain, w, wo, kc, vc):
    count, width = len(blocks), blocks[0].shape[1]
    row_count = sum(rows_out)
    vmem = pl.BlockSpec(memory_space=pltpu.VMEM)
    flops = 2 * row_count * (w.size + wo.size + 2 * kc.size)
    held = [pltpu.with_memory_space_constraint(x, pltpu.VMEM) for x in (gain, w, wo, kc, vc)]
    cache = pltpu.VMEM(kc.shape, kc.dtype)
    out = pl.pallas_call(
        functools.partial(block_kernel, count, len(rows_out)),
        out_shape=[jax.ShapeDtypeStruct((rows, width), jnp.bfloat16) for rows in rows_out]
        + [cache] * 2,
        in_specs=[pl.BlockSpec(memory_space=pltpu.SMEM)] + [vmem] * (count + 5),
        out_specs=[vmem] * (len(rows_out) + 2),
        input_output_aliases={count + 4: len(rows_out), count + 5: len(rows_out) + 1},
        scratch_shapes=[
            pltpu.VMEM((row_count, width), jnp.bfloat16),
            pltpu.VMEM((row_count, kc.shape[1]), jnp.bfloat16),
        ],
        compiler_params=pltpu.CompilerParams(vmem_limit_bytes=VMEM_LIMIT),
        cost_estimate=pl.CostEstimate(
            flops=flops, bytes_accessed=2 * (w.size + wo.size), transcendentals=0
        ),
    )(info, *blocks, *held)
    return out[:-2], out[-2], out[-1]


STAY = ((0, 0), (1, 1), (2, 2), (3, 3))
NEAR = ((0, 1), (1, 0), (2, 3), (3, 2))
FAR = ((0, 3), (1, 2), (2, 1), (3, 0))
CROSS = ((0, 2), (1, 3), (2, 0), (3, 1))


def send(block, pairs, hop=0):
    sections = lax.axis_size("section")
    n = lax.axis_size("uly")
    route = [
        (s * n + a, (s + hop) % sections * n + b) for s in range(sections) for a, b in pairs
    ]
    return lax.ppermute(block, ("section", "uly"), route)


def summed(*blocks):
    total = blocks[0].astype(jnp.float32)
    for block in blocks[1:]:
        total = total + block.astype(jnp.float32)
    return total


def summed(*blocks):
    total = blocks[0].astype(jnp.float32)
    for block in blocks[1:]:
        total = total + block.astype(jnp.float32)
    return total


def rounded(*blocks):
    return summed(*blocks).astype(jnp.bfloat16)


def behind(block, other):
    return lax.optimization_barrier((block, other))[0]


def cut(blocks, sizes):
    whole = jnp.concatenate(blocks)
    starts = [sum(sizes[:i]) for i in range(len(sizes))]
    return [whole[start:start + size] for start, size in zip(starts, sizes)]


def gathered(own, low):
    far = send(own, FAR)
    near = send(own, NEAR)
    last = send(far, NEAR)
    kept = [jnp.where(low, own, far), jnp.where(low, far, own)]
    return kept, [jnp.where(low, near, last), jnp.where(low, last, near)]


def passed_on(kept, terms):
    count = len(kept)
    next_kept, next_others = [], []
    pair = None
    for current, mine, partners in zip(kept, terms[:count], terms[count:]):
        partners = partners if pair is None else behind(partners, pair)
        pair = rounded(mine, send(partners, NEAR))
        updated = rounded(current, pair, send(pair, FAR))
        next_others.append(send(updated, NEAR))
        next_kept.append(updated)
    return next_kept, next_others


def delivered(kept, terms, low):
    first, second, near_first, near_second = terms
    before = jnp.where(low, *cut(kept, [first.shape[0], second.shape[0]]))
    cross = send(jnp.where(low, near_second, near_first), CROSS, 1)
    far = send(jnp.where(low, second, first), FAR, 1)
    near = send(jnp.where(low, near_first, near_second), NEAR, 1)
    base = send(rounded(before, jnp.where(low, first, second)), STAY, 1)
    total = lax.optimization_barrier(summed(cross))
    for block in (far, near):
        total = lax.optimization_barrier(total + block.astype(jnp.float32))
    return (total + base.astype(jnp.float32)).astype(jnp.bfloat16)


def shards(
    state, patch_slot, section_active, qkv_weight, out_weight, norm_gain, stale_keys, stale_values
):
    section_count = lax.axis_size("section")
    section_index = lax.axis_index("section")
    block_count = section_active[0]
    n = lax.axis_size("uly")
    low = lax.axis_index("uly") < n // 2
    shard_rows = state.shape[1]
    patch_rows = shard_rows * n
    stored = (
        jnp.transpose(qkv_weight[0], (1, 0, 2)),
        out_weight[0],
        stale_keys[0],
        stale_values[0],
        norm_gain,
    )
    w, wo, kc, vc, gain = loaded(*stored)
    kept, others = gathered(state[0], low)
    for tick in range(TICKS):
        slot = patch_slot[(section_index - tick) % section_count]
        for index in range(PASSES):
            applies = block_count > index
            info = jnp.stack([slot * patch_rows, applies.astype(jnp.int32)])
            last = index == PASSES - 1
            final = last and tick == TICKS - 1
            terms, kc, vc = block_terms(info, kept + others, [shard_rows] * n, gain, w, wo, kc, vc)
            if final:
                return delivered(kept, terms, low)[None]
            if last:
                kept, others = gathered(delivered(kept, terms, low), low)
            else:
                kept, others = passed_on(kept, terms)


def solution(mesh):
    return jax.shard_map(
        shards,
        mesh=mesh,
        in_specs=(
            P("section", "uly", None),
            P(),
            P("section"),
            P("section", None, None, "uly"),
            P("section", "uly", None),
            P("section", None),
            P("section", None, "uly"),
            P("section", None, "uly"),
        ),
        out_specs=P("section", "uly", None),
        check_vma=False,
    )
```
